512 devices in a mesh: gx: 16 (over z, x_hi), gy: 32 (over x_lo, y, core).
Axes of the slice: x: 4 (x_hi: 2, x_lo: 2; x = x_hi * 2 + x_lo), y: 8, z: 8, core: 2. Of those that a mesh axis runs over, the one named last changes fastest.
Arguments:
- field: bfloat16 [128, 256, 2, 48], P('gx', 'gy'), may hold values from -6 to 6
- cotangent: bfloat16 [128, 256, 2, 48], P('gx', 'gy'), may hold values from -6 to 6
- weights: bfloat16 [7, 27, 48, 48], replicated, may hold values from -0.15625 to 0.15625
Outputs:
- grad_field: bfloat16 [128, 256, 2, 48], P('gx', 'gy')
- grad_weights: float32 [7, 27, 48, 48], replicated
The draws below stay inside these ranges and needn't reach their ends.
All inputs are finite; a program needn't handle non-finite values.
Results may differ from the reference program's by a relative error of at most 0.02.
Values may be sent and summed in bfloat16 or wider, within the bound.
A program may use at most 64 MiB of HBM per device.

```python
import jax
import jax.numpy as jnp

C = 48
LAYERS = 7
Z = 2
NX = 128
NY = 256


def levels(own_key, dims, cuts, least, top_value):
    level = 1.0
    for dim, shards_of in cuts:
        draws = jax.random.uniform(jax.random.fold_in(jax.random.fold_in(own_key, 6), dim), (shards_of,), jnp.float32, least / len(cuts), top_value / len(cuts))
        level = level * jnp.repeat(jnp.exp(draws), dims[dim] // shards_of).reshape((-1,) + (1,) * (len(dims) - 1 - dim))
    return level


def noise(key, dims, width, limit, split=(), kind=jnp.bfloat16):
    drawn = width * jax.random.normal(key, dims, jnp.float32)
    if split:
        drawn = drawn * levels(key, dims, split, -0.22, 0.18)
    return jnp.clip(drawn, -limit, limit).astype(kind)


def setup_inputs(seed: int = 0) -> dict:
    seeds = jax.random.split(jax.random.key(seed), 4)
    field = noise(seeds[0], (NX, NY, Z, C), 1.0, 6.0, ((0, 16), (1, 32)))
    cotangent = noise(seeds[1], (NX, NY, Z, C), 1.0, 6.0, ((0, 16), (1, 32)))
    weights = noise(seeds[2], (LAYERS, 27, C, C), (27 * C) ** -0.5, 0.15625)
    return dict(field=field, cotangent=cotangent, weights=weights)


dilations = (1, 2, 4, 8, 4, 2, 1)


def shifted(values, along_x, along_y, along_z):
    rolled = jnp.roll(values, (-along_x, -along_y), axis=(0, 1))
    padded = jnp.pad(rolled, ((0, 0), (0, 0), (1, 1), (0, 0)))
    return padded[:, :, 1 + along_z:1 + along_z + Z]


def reference(field, cotangent, weights):
    states = [field]
    activs = []
    state = field
    for layer in range(LAYERS):
        spread = dilations[layer]
        activ = jax.nn.silu(state.astype(jnp.float32)).astype(jnp.bfloat16)
        activs.append(activ)
        total = state.astype(jnp.float32)
        for step_x in range(3):
            for step_y in range(3):
                for step_z in range(3):
                    index = step_x * 9 + step_y * 3 + step_z
                    moved = shifted(activ, (step_x - 1) * spread, (step_y - 1) * spread, step_z - 1)
                    total = total + jnp.dot(moved, weights[layer, index], preferred_element_type=jnp.float32)
        state = total.astype(jnp.bfloat16)
        states.append(state)
    grad = cotangent
    pieces = [None] * LAYERS
    for layer in reversed(range(LAYERS)):
        spread = dilations[layer]
        activ = activs[layer]
        flat_grad = grad.reshape(-1, C)
        taps = []
        back = jnp.zeros(grad.shape, jnp.float32)
        for step_x in range(3):
            for step_y in range(3):
                for step_z in range(3):
                    index = step_x * 9 + step_y * 3 + step_z
                    moved = shifted(activ, (step_x - 1) * spread, (step_y - 1) * spread, step_z - 1)
                    taps.append(jnp.dot(moved.reshape(-1, C).T, flat_grad, preferred_element_type=jnp.float32))
                    other = shifted(grad, (1 - step_x) * spread, (1 - step_y) * spread, 1 - step_z)
                    back = back + jnp.dot(other, weights[layer, index].T, preferred_element_type=jnp.float32)
        pieces[layer] = jnp.stack(taps)
        before = states[layer].astype(jnp.float32)
        sigma = jax.nn.sigmoid(before)
        grad = (grad.astype(jnp.float32) + sigma * (1.0 + before * (1.0 - sigma)) * back).astype(jnp.bfloat16)
    return grad, jnp.stack(pieces)
```

```python
import functools

import jax
import jax.numpy as jnp
from jax import lax
from jax.experimental import pallas as pl
from jax.experimental.pallas import tpu as pltpu
from jax.sharding import PartitionSpec as P

MESH = pl.DeviceIdType.MESH
bf16, f32 = jnp.bfloat16, jnp.float32
dilations = (1, 2, 4, 8, 4, 2, 1)
offsets = [(i, j) for i in (-1, 0, 1) for j in (-1, 0, 1)]
around = [o for o in offsets if o != (0, 0)]
layer_rows = 480
total_rows = 2048


def plan(size_x, size_y):
    if (size_x, size_y) == (16, 32):
        first = [(1, 0), (1, 1), (1, 4), (0, 1)]
        second = [(0, 0), (1, 2), (1, 3)]
        third = [(0, 2), (0, 3)]
    else:
        bits = [(0, b) for b in range(size_x.bit_length() - 1)] + [(1, b) for b in range(size_y.bit_length() - 1)]
        third, second, first = [bits[0]], [bits[1]], bits[2:]
    return first, second, third


def own_index(group, place):
    index = 0
    for position, (axis, bit) in enumerate(group):
        index = index + (place[axis] // 2**bit) % 2 * 2**position
    return index


def partner(group, place, mask):
    coords = list(place)
    index = 0
    for position, (axis, bit) in enumerate(group):
        mine = (place[axis] // 2**bit) % 2
        if mask >> position & 1:
            coords[axis] = coords[axis] + (1 - 2 * mine) * 2**bit
            mine = 1 - mine
        index = index + mine * 2**position
    return tuple(coords), index


def kernel(
    size_x, size_y,
    own_ref, w_any, grad_ref, packed_any,
    w_raw, w_wide, near, sent, region, high1, high2, high5, high_own, acts, cols,
    stage, land1, part1, land2, part2, land3, gathered,
    w_sem, near_send, near_recv, sum_send, sum_recv, out_sem,
):
    first, second, third = plan(size_x, size_y)
    place = (lax.axis_index("gx"), lax.axis_index("gy"))
    count1, count2, count3 = 2 ** len(first), 2 ** len(second), 2 ** len(third)
    chunk = total_rows // count1
    grain = chunk // count2

    def neighbour(i, j):
        return (
            lax.rem(place[0] + i + size_x, size_x),
            lax.rem(place[1] + j + size_y, size_y),
        )

    w_copy = pltpu.make_async_copy(w_any, w_raw, w_sem)
    w_copy.start()
    barrier = pltpu.get_barrier_semaphore()
    for i, j in around:
        pl.semaphore_signal(barrier, inc=1, device_id=neighbour(i, j), device_id_type=MESH)
    for group, count in ((first, count1), (second, count2), (third, count3)):
        for mask in range(1, count):
            pl.semaphore_signal(
                barrier, inc=1, device_id=partner(group, place, mask)[0], device_id_type=MESH
            )
    region[...] = jnp.zeros_like(region)
    w_wide[...] = jnp.zeros_like(w_wide)
    for group in range(2):
        stage[group, total_rows - 640 :] = jnp.zeros((640, 128), bf16)
    pl.semaphore_wait(barrier, 8 + count1 + count2 + count3 - 3)

    def exchange(number, source):
        for slot, (i, j) in enumerate(around):
            pltpu.make_async_remote_copy(
                src_ref=source,
                dst_ref=near.at[number, 7 - slot],
                send_sem=near_send.at[number],
                recv_sem=near_recv.at[number],
                device_id=neighbour(i, j),
                device_id_type=MESH,
            ).start()

    def send(number, block):
        sent[number] = block
        exchange(number, sent.at[number])

    def arrived(number):
        landed = near.at[number]
        pltpu.make_async_copy(landed, landed, near_recv.at[number]).wait()

    def spread_out(slot, number, own, change):
        for i, j in offsets:
            block = own if (i, j) == (0, 0) else near[number, around.index((i, j))].astype(f32)
            region[slot, 8 * (i + 1) : 8 * (i + 2), 8 * (j + 2) : 8 * (j + 3), :] = change(
                block
            ).reshape(8, 8, 128)

    def rounded(value):
        return value.astype(bf16).astype(f32)

    def silu(value):
        return rounded(value * jax.nn.sigmoid(value))

    def slope(value):
        sigma = jax.nn.sigmoid(value)
        return sigma * (1.0 + value * (1.0 - sigma))

    def box(slot, x, y, extent_x, extent_y):
        return region[slot, x : x + extent_x, y + 8 : y + 8 + extent_y, :].reshape(
            extent_x * extent_y, 128
        )

    def put(slot, x, y, extent_x, extent_y, value):
        region[slot, x : x + extent_x, y + 8 : y + 8 + extent_y, :] = value.reshape(
            extent_x, extent_y, 128
        )

    def fill(slot, spread, x, y, extent_x, extent_y):
        rows = extent_x * extent_y
        for index, (i, j) in enumerate(offsets):
            cols[:rows, index * 128 : (index + 1) * 128] = box(
                slot, x + i * spread, y + j * spread, extent_x, extent_y
            ).astype(bf16)
        return rows

    def forward(layer, rows):
        return jnp.dot(cols[:rows], w_wide[layer], preferred_element_type=f32)

    def backward(layer, rows):
        total = None
        for index in range(9):
            term = lax.dot_general(
                cols[:rows, index * 128 : (index + 1) * 128],
                w_wide[layer, index * 128 : (index + 1) * 128],
                (((1,), (1,)), ((), ())),
                preferred_element_type=f32,
            )
            total = term if total is None else total + term
        return total

    lane = lax.broadcasted_iota(jnp.int32, (48, 128), 1)

    def roll(value, left):
        return pltpu.roll(value, (128 - left) % 128, 1) if left % 128 else value

    def pack(group, slot, layers, layer):
        turned = jnp.transpose(acts[layer].astype(f32)).astype(bf16)
        base = slot * layer_rows
        rest = None
        for index in range(9):
            shifted = cols[:64, index * 128 : (index + 1) * 128]
            piece = jnp.dot(turned, shifted, preferred_element_type=f32)
            low, high = piece[:48], piece[48:96]
            moved = roll(high, 48)
            main = low + jnp.where((lane >= 48) & (lane < 96), 0.0, moved)
            stage[group, base + index * 48 : base + (index + 1) * 48] = main.astype(bf16)
            tail = jnp.where(lane < 16, high, 0.0)
            if index < 8:
                tail = roll(tail, 128 - 16 * index)
                rest = tail if rest is None else rest + tail
            else:
                last = roll(tail, 128 - 16 * slot)
        stage[group, base + 432 : base + 480] = rest.astype(bf16)
        shared = slice(layers * layer_rows, layers * layer_rows + 48)
        if slot:
            last = last + stage[group, shared].astype(f32)
        stage[group, shared] = last.astype(bf16)

    index1, index2 = own_index(first, place), own_index(second, place)

    def piece_of(index):
        return pl.ds(pl.multiple_of(index * chunk, chunk), chunk)

    def grain_of(index):
        return pl.ds(pl.multiple_of(index * grain, grain), grain)

    def copies(group, phase, members, source, target):
        for mask in range(1, 2 ** len(members)):
            device, index = partner(members, place, mask)
            pltpu.make_async_remote_copy(
                src_ref=source(index),
                dst_ref=target(mask),
                send_sem=sum_send.at[group, phase],
                recv_sem=sum_recv.at[group, phase],
                device_id=device,
                device_id_type=MESH,
            ).start()

    def landed(group, phase, ref):
        pltpu.make_async_copy(ref, ref, sum_recv.at[group, phase]).wait()

    def sum1_send(group):
        copies(
            group, 0, first,
            lambda index: stage.at[group, piece_of(index)],
            lambda mask: land1.at[group, mask - 1],
        )

    def sum1_wait(group):
        landed(group, 0, land1.at[group])
        total = stage[group, piece_of(index1)].astype(f32)
        for mask in range(1, count1):
            total = total + land1[group, mask - 1].astype(f32)
        part1[group] = total.astype(bf16)
        copies(
            group, 1, second,
            lambda index: part1.at[group, grain_of(index)],
            lambda mask: land2.at[group, mask - 1],
        )

    def sum2_wait(group):
        landed(group, 1, land2.at[group])
        total = part1[group, grain_of(index2)].astype(f32)
        for mask in range(1, count2):
            total = total + land2[group, mask - 1].astype(f32)
        part2[group] = total.astype(bf16)
        copies(
            group, 2, third,
            lambda index: part2.at[group],
            lambda mask: land3.at[group, mask - 1],
        )

    def sum3_wait(group):
        landed(group, 2, land3.at[group])
        terms = [part2[group].astype(f32)] + [
            land3[group, mask - 1].astype(f32) for mask in range(1, count3)
        ]
        while len(terms) > 1:
            terms = [a + b for a, b in zip(terms[::2], terms[1::2])]
        mine = gathered.at[group, index1, grain_of(index2)]
        mine[...] = terms[0].astype(bf16)
        copies(group, 3, second, lambda index: mine, lambda mask: mine)

    def gather_wait(group):
        grains = gathered.at[group, 0, pl.ds(0, grain * (count2 - 1))]
        landed(group, 3, grains)
        mine = gathered.at[group, index1]
        copies(group, 4, first, lambda index: mine, lambda mask: mine)

    def finish(group):
        landed(group, 4, gathered.at[group, pl.ds(0, count1 - 1)])
        copy = pltpu.make_async_copy(gathered.at[group], packed_any.at[group], out_sem.at[group])
        copy.start()
        return copy

    exchange(0, own_ref.at[0])
    exchange(6, own_ref.at[1])
    w_copy.wait()
    zeros32 = jnp.zeros((48, 32), f32)

    def widen(layer, carry):
        for index in range(9):
            minus, same, plus = (w_raw[layer, 3 * index + k].astype(f32) for k in range(3))
            w_wide[layer, index * 128 : index * 128 + 48] = jnp.concatenate(
                [same, minus, zeros32], axis=1
            ).astype(bf16)
            w_wide[layer, index * 128 + 48 : index * 128 + 96] = jnp.concatenate(
                [plus, same, zeros32], axis=1
            ).astype(bf16)
        return carry

    lax.fori_loop(0, 7, widen, 0)

    high0 = own_ref[0].astype(f32)
    acts[0] = silu(high0).astype(bf16)
    arrived(0)
    spread_out(0, 0, high0, lambda value: value)
    spread_out(1, 0, high0, silu)
    rows = fill(1, 1, 2, 0, 20, 24)
    value = rounded(box(0, 2, 0, 20, 24) + forward(0, rows))
    put(0, 2, 0, 20, 24, value)
    put(1, 2, 0, 20, 24, silu(value))
    high1[...] = box(0, 7, 4, 10, 16)
    acts[1] = box(1, 8, 8, 8, 8).astype(bf16)
    rows = fill(1, 2, 4, 4, 16, 16)
    value = rounded(box(0, 4, 4, 16, 16) + forward(1, rows))
    put(0, 4, 4, 16, 16, value)
    put(1, 4, 4, 16, 16, silu(value))
    high2[...] = box(0, 5, 4, 14, 16)
    acts[2] = box(1, 8, 8, 8, 8).astype(bf16)
    rows = fill(1, 4, 8, 8, 8, 8)
    high3 = rounded(box(0, 8, 8, 8, 8) + forward(2, rows))
    high_own[0] = high3
    active = silu(high3).astype(bf16)
    acts[3] = active
    send(1, active)
    arrived(1)

    def fill_blocks(number, own):
        for index, (i, j) in enumerate(offsets):
            block = own if (i, j) == (0, 0) else near[number, around.index((i, j))]
            cols[:64, index * 128 : (index + 1) * 128] = block

    fill_blocks(1, acts[3])
    high4 = rounded(high_own[0] + forward(3, 64))
    high_own[1] = high4
    send(2, high4.astype(bf16))
    acts[4] = silu(high4).astype(bf16)
    arrived(6)
    spread_out(2, 6, own_ref[1].astype(f32), lambda value: value)
    arrived(2)
    spread_out(0, 2, high_own[1], lambda value: value)
    spread_out(1, 2, high_own[1], silu)
    rows = fill(1, 4, 4, 4, 16, 16)
    value = rounded(box(0, 4, 4, 16, 16) + forward(4, rows))
    high5[...] = value
    put(0, 4, 4, 16, 16, value)
    put(1, 4, 4, 16, 16, silu(value))
    acts[5] = box(1, 8, 8, 8, 8).astype(bf16)
    rows = fill(1, 2, 8, 8, 8, 8)
    high6 = rounded(box(0, 8, 8, 8, 8) + forward(5, rows))
    high_own[2] = high6
    acts[6] = silu(high6).astype(bf16)

    def fill_back(slot, spread, x, y, extent_x, extent_y):
        return fill(slot, -spread, x, y, extent_x, extent_y)

    rows = fill_back(2, 1, 8, 8, 8, 8)
    grad6 = (own_ref[1].astype(f32) + slope(high_own[2]) * backward(6, rows)).astype(bf16)
    send(3, grad6)
    pack(0, 0, 4, 6)
    arrived(3)
    spread_out(2, 3, sent[3].astype(f32), lambda value: value)
    rows = fill_back(2, 2, 4, 4, 16, 16)
    value = rounded(box(2, 4, 4, 16, 16) + slope(high5[...]) * backward(5, rows))
    put(0, 4, 4, 16, 16, value)
    rows = fill_back(0, 4, 8, 8, 8, 8)
    grad4 = (box(0, 8, 8, 8, 8) + slope(high_own[1]) * backward(4, rows)).astype(bf16)
    send(4, grad4)
    pack(0, 2, 4, 4)
    fill_back(2, 2, 8, 8, 8, 8)
    pack(0, 1, 4, 5)
    arrived(4)

    def fill_blocks_back(number, own):
        for index, (i, j) in enumerate(offsets):
            block = own if (i, j) == (0, 0) else near[number, around.index((-i, -j))]
            cols[:64, index * 128 : (index + 1) * 128] = block

    fill_blocks_back(4, sent[4])
    grad3 = (sent[4].astype(f32) + slope(high_own[0]) * backward(3, 64)).astype(bf16)
    send(5, grad3)
    pack(0, 3, 4, 3)
    sum1_send(0)
    arrived(5)
    spread_out(2, 5, sent[5].astype(f32), lambda value: value)
    rows = fill_back(2, 4, 5, 4, 14, 16)
    value = rounded(box(2, 5, 4, 14, 16) + slope(high2[...]) * backward(2, rows))
    put(0, 5, 4, 14, 16, value)
    fill_back(2, 4, 8, 8, 8, 8)
    pack(1, 0, 3, 2)
    sum1_wait(0)
    rows = fill_back(0, 2, 7, 4, 10, 16)
    value = rounded(box(0, 7, 4, 10, 16) + slope(high1[...]) * backward(1, rows))
    put(1, 7, 4, 10, 16, value)
    fill_back(0, 2, 8, 8, 8, 8)
    pack(1, 1, 3, 1)
    rows = fill_back(1, 1, 8, 8, 8, 8)
    pack(1, 2, 3, 0)
    sum1_send(1)
    sum2_wait(0)
    grad_ref[...] = (
        box(1, 8, 8, 8, 8) + slope(own_ref[0].astype(f32)) * backward(0, rows)
    ).astype(bf16)
    sum3_wait(0)
    sum1_wait(1)
    gather_wait(0)
    sum2_wait(1)
    sum3_wait(1)
    gather_wait(1)
    out0 = finish(0)
    out1 = finish(1)
    for number in range(7):
        ref = near.at[number]
        pltpu.make_async_copy(ref, ref, near_send.at[number]).wait()
    for group in range(2):
        grains = gathered.at[group, 0, pl.ds(0, grain * (count2 - 1))]
        for phase, ref in enumerate(
            (land1.at[group], land2.at[group], land3.at[group], grains, gathered.at[group, pl.ds(0, count1 - 1)])
        ):
            pltpu.make_async_copy(ref, ref, sum_send.at[group, phase]).wait()
    out0.wait()
    out1.wait()


def unpack(packed_ref, shared_ref, out_ref):
    step = pl.program_id(0)
    lane = lax.broadcasted_iota(jnp.int32, (48, 128), 1)
    rest = packed_ref[432:480].astype(f32)
    shared = shared_ref[...].astype(f32)
    slot = jnp.where(step < 3, 2 - step, 6 - step)
    last = pltpu.roll(shared, lax.rem(128 - 16 * slot, 128), 1)
    for index in range(9):
        main = packed_ref[index * 48 : (index + 1) * 48].astype(f32)
        if index == 8:
            tail = last
        elif index:
            tail = pltpu.roll(rest, 128 - 16 * index, 1)
        else:
            tail = rest
        plus = jnp.where(lane < 16, tail, pltpu.roll(main, 48, 1))
        out_ref[3 * index] = pltpu.roll(main, 80, 1)[:, :48]
        out_ref[3 * index + 1] = main[:, :48]
        out_ref[3 * index + 2] = plus[:, :48]


def on_device(field, cotangent, weights):
    size_x, size_y = lax.axis_size("gx"), lax.axis_size("gy")
    first, second, third = plan(size_x, size_y)
    count1, count2, count3 = 2 ** len(first), 2 ** len(second), 2 ** len(third)
    chunk = total_rows // count1
    grain = chunk // count2
    own = jnp.stack([field, cotangent]).reshape(2, 64, 96)
    own = jnp.pad(own, ((0, 0), (0, 0), (0, 32)))
    vmem = pl.BlockSpec(memory_space=pltpu.VMEM)
    grad, packed = pl.pallas_call(
        functools.partial(kernel, size_x, size_y),
        out_shape=(
            jax.ShapeDtypeStruct((64, 128), bf16),
            jax.ShapeDtypeStruct((2, count1, chunk, 128), bf16),
        ),
        in_specs=[vmem, pl.BlockSpec(memory_space=pl.ANY)],
        out_specs=(vmem, pl.BlockSpec(memory_space=pl.ANY)),
        scratch_shapes=[
            pltpu.VMEM((7, 27, 48, 48), bf16),
            pltpu.VMEM((7, 1152, 128), bf16),
            pltpu.VMEM((7, 8, 64, 128), bf16),
            pltpu.VMEM((6, 64, 128), bf16),
            pltpu.VMEM((3, 24, 40, 128), f32),
            pltpu.VMEM((160, 128), f32),
            pltpu.VMEM((224, 128), f32),
            pltpu.VMEM((256, 128), f32),
            pltpu.VMEM((3, 64, 128), f32),
            pltpu.VMEM((7, 64, 128), bf16),
            pltpu.VMEM((480, 1152), bf16),
            pltpu.VMEM((2, total_rows, 128), bf16),
            pltpu.VMEM((2, count1 - 1, chunk, 128), bf16),
            pltpu.VMEM((2, chunk, 128), bf16),
            pltpu.VMEM((2, count2 - 1, grain, 128), bf16),
            pltpu.VMEM((2, grain, 128), bf16),
            pltpu.VMEM((2, count3 - 1, grain, 128), bf16),
            pltpu.VMEM((2, count1, chunk, 128), bf16),
            pltpu.SemaphoreType.DMA,
            pltpu.SemaphoreType.DMA((7,)),
            pltpu.SemaphoreType.DMA((7,)),
            pltpu.SemaphoreType.DMA((2, 5)),
            pltpu.SemaphoreType.DMA((2, 5)),
            pltpu.SemaphoreType.DMA((2,)),
        ],
        compiler_params=pltpu.CompilerParams(
            collective_id=0, has_side_effects=True, vmem_limit_bytes=40 * 2**20
        ),
    )(own, weights)
    packed = packed.reshape(2, total_rows, 128)
    kernels = pl.pallas_call(
        unpack,
        grid=(7,),
        out_shape=jax.ShapeDtypeStruct((7, 27, 48, 48), f32),
        in_specs=[
            pl.BlockSpec(
                (None, pl.Element(480), pl.Element(128)),
                lambda step: (
                    jnp.where(step < 3, 1, 0),
                    480 * jnp.where(step < 3, 2 - step, 6 - step),
                    0,
                ),
            ),
            pl.BlockSpec(
                (None, pl.Element(48), pl.Element(128)),
                lambda step: (jnp.where(step < 3, 1, 0), jnp.where(step < 3, 1440, 1920), 0),
            ),
        ],
        out_specs=pl.BlockSpec((None, 27, 48, 48), lambda step: (step, 0, 0, 0)),
    )(packed, packed)
    return grad[:, :96].reshape(field.shape), kernels


def solution(mesh):
    in_specs = (P("gx", "gy", None, None), P("gx", "gy", None, None), P())
    out_specs = (P("gx", "gy", None, None), P())
    return jax.shard_map(
        on_device, mesh=mesh, in_specs=in_specs, out_specs=out_specs, check_vma=False
    )
```

```python
import functools

import jax
import jax.numpy as jnp
from jax import lax
from jax.experimental import pallas as pl
from jax.experimental.pallas import tpu as pltpu
from jax.sharding import PartitionSpec as P

MESH = pl.DeviceIdType.MESH
bf16, f32 = jnp.bfloat16, jnp.float32
dilations = (1, 2, 4, 8, 4, 2, 1)
offsets = [(i, j) for i in (-1, 0, 1) for j in (-1, 0, 1)]
around = [o for o in offsets if o != (0, 0)]
layer_rows = 480
groups = ((6, 5, 4, 3), (2, 1, 0))
group_rows = (2048, 1536)


def plan(size_x, size_y):
    if (size_x, size_y) == (16, 32):
        return [(1, 0), (1, 1), (1, 4), (0, 0), (0, 1)], [[(1, 2), (1, 3)], [(0, 2), (0, 3)]]
    return [(0, 0), (1, 0)], [[(0, 1)], [(1, 1)]]


def hosted(place, size_y):
    half = size_y // 2
    high, low, z = place[0] % 2, place[1] // half, place[0] // 2
    return place[0] // 2 * 2 + (high + z) % 2, (low + high) % 2 * half + place[1] % half


def host(block, size_y):
    half = size_y // 2
    z = block[0] // 2
    high = (block[0] % 2 + z) % 2
    return z * 2 + high, (block[1] // half + high) % 2 * half + block[1] % half


def own_index(group, place):
    index = 0
    for position, (axis, bit) in enumerate(group):
        index = index + (place[axis] // 2**bit) % 2 * 2**position
    return index


def partner(group, place, mask):
    coords = list(place)
    index = 0
    for position, (axis, bit) in enumerate(group):
        mine = (place[axis] // 2**bit) % 2
        if mask >> position & 1:
            coords[axis] = coords[axis] + (1 - 2 * mine) * 2**bit
            mine = 1 - mine
        index = index + mine * 2**position
    return tuple(coords), index


def kernel(
    size_x, size_y,
    field_any, cotangent_any, w_any, grad_ref, out_ref,
    raw, w_raw, own, w_wide, near, sent, region, high1, high2, high5, high_own, acts, cols, back_home, landed_home,
    *rest,
):
    first, mids = plan(size_x, size_y)
    count1 = 2 ** len(first)
    phases = len(mids) + 2
    buffers, (raw_sem, near_send, near_recv, home_sem, sum_send, sum_recv) = rest[:-6], rest[-6:]
    per_group = len(buffers) // 2
    stages, lands, gathers, parts, mid_lands = [], [], [], [], []
    for group in range(2):
        stage, land, gathered, *others = buffers[group * per_group : (group + 1) * per_group]
        stages.append(stage)
        lands.append(land)
        gathers.append(gathered)
        parts.append(others[::2])
        mid_lands.append(others[1::2])
    chunks = [rows // count1 for rows in group_rows]

    place = (lax.axis_index("gx"), lax.axis_index("gy"))
    mine = hosted(place, size_y)

    def step(at, i, j):
        return (at[0] + i + size_x) % size_x, (at[1] + j + size_y) % size_y

    def equal(a, b):
        return jnp.logical_and(a[0] == b[0], a[1] == b[1])

    def signal(device):
        pl.semaphore_signal(barrier, inc=1, device_id=device, device_id_type=MESH)

    loads = [
        pltpu.make_async_copy(field_any, raw.at[0], raw_sem.at[0]),
        pltpu.make_async_copy(cotangent_any, raw.at[1], raw_sem.at[1]),
        pltpu.make_async_copy(w_any, w_raw, raw_sem.at[2]),
    ]
    for load in loads:
        load.start()
    at_home = equal(mine, place)
    neighbours = {o: host(step(mine, *o), size_y) for o in around}
    targets = {o: host(step(place, *o), size_y) for o in offsets}
    kept = [equal(targets[o], place) for o in offsets]
    keeps = functools.reduce(jnp.logical_or, kept)
    barrier = pltpu.get_barrier_semaphore()
    for o in offsets:
        source = step(mine, *o)

        @pl.when(jnp.logical_not(equal(source, place)))
        def _():
            signal(source)

    for o in around:
        signal(neighbours[o])
    partners = 0
    for group in [first] + mids:
        for mask in range(1, 2 ** len(group)):
            signal(partner(group, place, mask)[0])
            partners += 1

    @pl.when(jnp.logical_not(at_home))
    def _():
        signal(host(place, size_y))

    region[...] = jnp.zeros_like(region)
    w_wide[...] = jnp.zeros_like(w_wide)
    for group in range(2):
        used = len(groups[group]) * layer_rows + 48
        stages[group][used:] = jnp.zeros((group_rows[group] - used, 128), bf16)
    for which in range(2):
        loads[which].wait()
        value = raw[which].astype(f32)
        planes = [value[:, :, z, :].reshape(64, 48) for z in range(2)]
        own[which] = jnp.concatenate(planes + [jnp.zeros((64, 32), f32)], axis=1).astype(bf16)
    pl.semaphore_wait(barrier, 8 + partners + jnp.where(keeps, 8, 9) + jnp.where(at_home, 0, 1))

    outward = sorted(around, key=lambda o: -abs(o[0]) - abs(o[1]))

    def scatter(number, source):
        for o in outward + [(0, 0)]:
            target = near.at[number, 7 - around.index(o) if o != (0, 0) else 8]

            @pl.when(jnp.logical_not(equal(targets[o], place)))
            def _():
                pltpu.make_async_remote_copy(
                    src_ref=source,
                    dst_ref=target,
                    send_sem=near_send.at[number],
                    recv_sem=near_recv.at[number],
                    device_id=targets[o],
                    device_id_type=MESH,
                ).start()

            @pl.when(equal(targets[o], place))
            def _():
                pltpu.make_async_copy(source, target, near_recv.at[number]).start()

    def exchange(number, source):
        for o in outward:
            pltpu.make_async_remote_copy(
                src_ref=source,
                dst_ref=near.at[number, 7 - around.index(o)],
                send_sem=near_send.at[number],
                recv_sem=near_recv.at[number],
                device_id=neighbours[o],
                device_id_type=MESH,
            ).start()

    def send(number, block):
        sent[number] = block
        exchange(number, sent.at[number])

    def arrived(number):
        landed = near.at[number, pl.ds(0, 9 if number in (0, 6) else 8)]
        pltpu.make_async_copy(landed, landed, near_recv.at[number]).wait()

    def spread_out(slot, number, own, change):
        for i, j in offsets:
            block = own if (i, j) == (0, 0) else near[number, around.index((i, j))].astype(f32)
            region[slot, 8 * (i + 1) : 8 * (i + 2), 8 * (j + 2) : 8 * (j + 3), :] = change(
                block
            ).reshape(8, 8, 128)

    def rounded(value):
        return value.astype(bf16).astype(f32)

    def silu(value):
        return rounded(value * jax.nn.sigmoid(value))

    def slope(value):
        sigma = jax.nn.sigmoid(value)
        return sigma * (1.0 + value * (1.0 - sigma))

    def box(slot, x, y, extent_x, extent_y):
        return region[slot, x : x + extent_x, y + 8 : y + 8 + extent_y, :].reshape(
            extent_x * extent_y, 128
        )

    def put(slot, x, y, extent_x, extent_y, value):
        region[slot, x : x + extent_x, y + 8 : y + 8 + extent_y, :] = value.reshape(
            extent_x, extent_y, 128
        )

    def fill(slot, spread, x, y, extent_x, extent_y):
        rows = extent_x * extent_y
        for index, (i, j) in enumerate(offsets):
            cols[:rows, index * 128 : (index + 1) * 128] = box(
                slot, x + i * spread, y + j * spread, extent_x, extent_y
            ).astype(bf16)
        return rows

    def forward(layer, rows):
        return jnp.dot(cols[:rows], w_wide[layer], preferred_element_type=f32)

    def backward(layer, rows):
        total = None
        for index in range(9):
            term = lax.dot_general(
                cols[:rows, index * 128 : (index + 1) * 128],
                w_wide[layer, index * 128 : (index + 1) * 128],
                (((1,), (1,)), ((), ())),
                preferred_element_type=f32,
            )
            total = term if total is None else total + term
        return total

    lane = lax.broadcasted_iota(jnp.int32, (48, 128), 1)

    def roll(value, left):
        return pltpu.roll(value, (128 - left) % 128, 1) if left % 128 else value

    def pack(layer):
        group = 0 if layer in groups[0] else 1
        slot, layers, stage = groups[group].index(layer), len(groups[group]), stages[group]
        turned = jnp.transpose(acts[layer].astype(f32)).astype(bf16)
        base = slot * layer_rows
        rest = None
        for index in range(9):
            shifted = cols[:64, index * 128 : (index + 1) * 128]
            piece = jnp.dot(turned, shifted, preferred_element_type=f32)
            low, high = piece[:48], piece[48:96]
            moved = roll(high, 48)
            main = low + jnp.where((lane >= 48) & (lane < 96), 0.0, moved)
            stage[base + index * 48 : base + (index + 1) * 48] = main.astype(bf16)
            tail = jnp.where(lane < 16, high, 0.0)
            if index < 8:
                tail = roll(tail, 128 - 16 * index)
                rest = tail if rest is None else rest + tail
            else:
                last = roll(tail, 128 - 16 * slot)
        stage[base + 432 : base + 480] = rest.astype(bf16)
        shared = slice(layers * layer_rows, layers * layer_rows + 48)
        if slot:
            last = last + stage[shared].astype(f32)
        stage[shared] = last.astype(bf16)

    index1 = own_index(first, place)

    def piece_of(group, index):
        return pl.ds(pl.multiple_of(index * chunks[group], chunks[group]), chunks[group])

    def copies(group, phase, members, source, target):
        for mask in reversed(range(1, 2 ** len(members))):
            device, index = partner(members, place, mask)
            pltpu.make_async_remote_copy(
                src_ref=source(index),
                dst_ref=target(mask),
                send_sem=sum_send.at[group, phase],
                recv_sem=sum_recv.at[group, phase],
                device_id=device,
                device_id_type=MESH,
            ).start()

    def received(group, phase):
        if phase == 0:
            return lands[group]
        if phase < phases - 1:
            return mid_lands[group][phase - 1]
        return gathers[group].at[pl.ds(0, (count1 - 1) * chunks[group])]

    def landed(group, phase):
        ref = received(group, phase)
        pltpu.make_async_copy(ref, ref, sum_recv.at[group, phase]).wait()

    def sum_send_first(group):
        copies(
            group, 0, first,
            lambda index: stages[group].at[piece_of(group, index)],
            lambda mask: lands[group].at[mask - 1],
        )

    def sum_step(group, phase):
        landed(group, phase)
        if phase == 0:
            terms = [stages[group][piece_of(group, index1)].astype(f32)]
            land, count = lands[group], count1
        else:
            terms = [parts[group][phase - 1][...].astype(f32)]
            land, count = mid_lands[group][phase - 1], 2 ** len(mids[phase - 1])
        terms += [land[mask - 1].astype(f32) for mask in range(1, count)]
        while len(terms) > 1:
            terms = [a + b for a, b in zip(terms[::2], terms[1::2])]
        total = terms[0].astype(bf16)
        if phase < len(mids):
            part = parts[group][phase]
            part[...] = total
            copies(
                group, phase + 1, mids[phase],
                lambda index: part,
                lambda mask: mid_lands[group][phase].at[mask - 1],
            )
        else:
            gathers[group][piece_of(group, index1)] = total
            whole = gathers[group].at[piece_of(group, index1)]
            copies(group, phase + 1, first, lambda index: whole, lambda mask: whole)

    def unpack(group):
        packed = gathers[group]
        shared = len(groups[group]) * layer_rows
        shared = packed[shared : shared + 48].astype(f32)
        for slot, layer in enumerate(groups[group]):
            base = slot * layer_rows
            rest = packed[base + 432 : base + 480].astype(f32)
            for index in range(9):
                main = packed[base + index * 48 : base + (index + 1) * 48].astype(f32)
                tail = roll(rest, 16 * index) if index < 8 else roll(shared, 16 * slot)
                plus = jnp.where(lane < 16, tail, roll(main, 80))
                out_ref[layer, 3 * index] = roll(main, 48)[:, :48].astype(bf16)
                out_ref[layer, 3 * index + 1] = main[:, :48].astype(bf16)
                out_ref[layer, 3 * index + 2] = plus[:, :48].astype(bf16)

    scatter(0, own.at[0])
    scatter(6, own.at[1])
    loads[2].wait()
    zeros32 = jnp.zeros((48, 32), f32)

    def widen(layer, carry):
        for index in range(9):
            minus, same, plus = (w_raw[layer, 3 * index + k].astype(f32) for k in range(3))
            w_wide[layer, index * 128 : index * 128 + 48] = jnp.concatenate(
                [same, minus, zeros32], axis=1
            ).astype(bf16)
            w_wide[layer, index * 128 + 48 : index * 128 + 96] = jnp.concatenate(
                [plus, same, zeros32], axis=1
            ).astype(bf16)
        return carry

    lax.fori_loop(0, 7, widen, 0)

    arrived(0)
    high0 = near[0, 8].astype(f32)
    acts[0] = silu(high0).astype(bf16)
    spread_out(0, 0, high0, lambda value: value)
    spread_out(1, 0, high0, silu)
    rows = fill(1, 1, 2, 0, 20, 24)
    value = rounded(box(0, 2, 0, 20, 24) + forward(0, rows))
    put(0, 2, 0, 20, 24, value)
    put(1, 2, 0, 20, 24, silu(value))
    high1[...] = box(0, 7, 4, 10, 16)
    acts[1] = box(1, 8, 8, 8, 8).astype(bf16)
    rows = fill(1, 2, 4, 4, 16, 16)
    value = rounded(box(0, 4, 4, 16, 16) + forward(1, rows))
    put(0, 4, 4, 16, 16, value)
    put(1, 4, 4, 16, 16, silu(value))
    high2[...] = box(0, 5, 4, 14, 16)
    acts[2] = box(1, 8, 8, 8, 8).astype(bf16)
    rows = fill(1, 4, 8, 8, 8, 8)
    high3 = rounded(box(0, 8, 8, 8, 8) + forward(2, rows))
    high_own[0] = high3
    active = silu(high3).astype(bf16)
    acts[3] = active
    send(1, active)
    arrived(1)

    def fill_blocks(number, own):
        for index, (i, j) in enumerate(offsets):
            block = own if (i, j) == (0, 0) else near[number, around.index((i, j))]
            cols[:64, index * 128 : (index + 1) * 128] = block

    fill_blocks(1, acts[3])
    high4 = rounded(high_own[0] + forward(3, 64))
    high_own[1] = high4
    send(2, high4.astype(bf16))
    acts[4] = silu(high4).astype(bf16)
    arrived(6)
    spread_out(2, 6, near[6, 8].astype(f32), lambda value: value)
    arrived(2)
    spread_out(0, 2, high_own[1], lambda value: value)
    spread_out(1, 2, high_own[1], silu)
    rows = fill(1, 4, 4, 4, 16, 16)
    value = rounded(box(0, 4, 4, 16, 16) + forward(4, rows))
    high5[...] = value
    put(0, 4, 4, 16, 16, value)
    put(1, 4, 4, 16, 16, silu(value))
    acts[5] = box(1, 8, 8, 8, 8).astype(bf16)
    rows = fill(1, 2, 8, 8, 8, 8)
    high6 = rounded(box(0, 8, 8, 8, 8) + forward(5, rows))
    high_own[2] = high6
    acts[6] = silu(high6).astype(bf16)

    def fill_back(slot, spread, x, y, extent_x, extent_y):
        return fill(slot, -spread, x, y, extent_x, extent_y)

    rows = fill_back(2, 1, 8, 8, 8, 8)
    grad6 = (near[6, 8].astype(f32) + slope(high_own[2]) * backward(6, rows)).astype(bf16)
    send(3, grad6)
    pack(6)
    arrived(3)
    spread_out(2, 3, sent[3].astype(f32), lambda value: value)
    rows = fill_back(2, 2, 4, 4, 16, 16)
    value = rounded(box(2, 4, 4, 16, 16) + slope(high5[...]) * backward(5, rows))
    put(0, 4, 4, 16, 16, value)
    rows = fill_back(0, 4, 8, 8, 8, 8)
    grad4 = (box(0, 8, 8, 8, 8) + slope(high_own[1]) * backward(4, rows)).astype(bf16)
    send(4, grad4)
    pack(4)
    fill_back(2, 2, 8, 8, 8, 8)
    pack(5)
    arrived(4)

    def fill_blocks_back(number, own):
        for index, (i, j) in enumerate(offsets):
            block = own if (i, j) == (0, 0) else near[number, around.index((-i, -j))]
            cols[:64, index * 128 : (index + 1) * 128] = block

    fill_blocks_back(4, sent[4])
    grad3 = (sent[4].astype(f32) + slope(high_own[0]) * backward(3, 64)).astype(bf16)
    send(5, grad3)
    pack(3)
    sum_send_first(0)
    arrived(5)
    spread_out(2, 5, sent[5].astype(f32), lambda value: value)
    rows = fill_back(2, 4, 5, 4, 14, 16)
    value = rounded(box(2, 5, 4, 14, 16) + slope(high2[...]) * backward(2, rows))
    put(0, 5, 4, 14, 16, value)
    fill_back(2, 4, 8, 8, 8, 8)
    pack(2)
    rows = fill_back(0, 2, 7, 4, 10, 16)
    value = rounded(box(0, 7, 4, 10, 16) + slope(high1[...]) * backward(1, rows))
    put(1, 7, 4, 10, 16, value)
    fill_back(0, 2, 8, 8, 8, 8)
    pack(1)
    sum_step(0, 0)
    rows = fill_back(1, 1, 8, 8, 8, 8)
    pack(0)
    sum_send_first(1)
    back_home[...] = (
        box(1, 8, 8, 8, 8) + slope(near[0, 8].astype(f32)) * backward(0, rows)
    ).astype(bf16)
    to_owner = pltpu.make_async_remote_copy(
        src_ref=back_home,
        dst_ref=landed_home,
        send_sem=home_sem.at[0],
        recv_sem=home_sem.at[1],
        device_id=mine,
        device_id_type=MESH,
    )

    @pl.when(jnp.logical_not(at_home))
    def _():
        to_owner.start()

    @pl.when(at_home)
    def _():
        landed_home[...] = back_home[...]

    for phase in range(1, phases - 1):
        sum_step(0, phase)
        sum_step(1, phase - 1)
    sum_step(1, phases - 2)

    @pl.when(jnp.logical_not(at_home))
    def _():
        to_owner.wait()

    grad_ref[...] = landed_home[...]
    for number in range(1, 6):
        ref = near.at[number, pl.ds(0, 8)]
        pltpu.make_async_copy(ref, ref, near_send.at[number]).wait()
    for number in (0, 6):
        for count, chosen in ((8, keeps), (9, jnp.logical_not(keeps))):

            @pl.when(chosen)
            def _():
                ref = near.at[number, pl.ds(0, count)]
                pltpu.make_async_copy(ref, ref, near_send.at[number]).wait()

    landed(0, phases - 1)
    unpack(0)
    landed(1, phases - 1)
    unpack(1)
    for group in range(2):
        for phase in range(phases):
            ref = received(group, phase)
            pltpu.make_async_copy(ref, ref, sum_send.at[group, phase]).wait()


def on_device(field, cotangent, weights):
    size_x, size_y = lax.axis_size("gx"), lax.axis_size("gy")
    first, mids = plan(size_x, size_y)
    count1 = 2 ** len(first)
    vmem = pl.BlockSpec(memory_space=pltpu.VMEM)
    anywhere = pl.BlockSpec(memory_space=pl.ANY)
    buffers = []
    for rows in group_rows:
        chunk = rows // count1
        buffers += [
            pltpu.VMEM((rows, 128), bf16),
            pltpu.VMEM((count1 - 1, chunk, 128), bf16),
            pltpu.VMEM((rows, 128), bf16),
        ]
        for members in mids:
            buffers += [
                pltpu.VMEM((chunk, 128), bf16),
                pltpu.VMEM((2 ** len(members) - 1, chunk, 128), bf16),
            ]
    phases = len(mids) + 2
    grad, kernels = pl.pallas_call(
        functools.partial(kernel, size_x, size_y),
        out_shape=(
            jax.ShapeDtypeStruct((64, 128), bf16),
            jax.ShapeDtypeStruct(weights.shape, bf16),
        ),
        in_specs=[anywhere] * 3,
        out_specs=(vmem, vmem),
        scratch_shapes=[
            pltpu.VMEM((2,) + field.shape, bf16),
            pltpu.VMEM(weights.shape, bf16),
            pltpu.VMEM((2, 64, 128), bf16),
            pltpu.VMEM((7, 1152, 128), bf16),
            pltpu.VMEM((7, 9, 64, 128), bf16),
            pltpu.VMEM((6, 64, 128), bf16),
            pltpu.VMEM((3, 24, 40, 128), f32),
            pltpu.VMEM((160, 128), f32),
            pltpu.VMEM((224, 128), f32),
            pltpu.VMEM((256, 128), f32),
            pltpu.VMEM((3, 64, 128), f32),
            pltpu.VMEM((7, 64, 128), bf16),
            pltpu.VMEM((480, 1152), bf16),
            pltpu.VMEM((64, 128), bf16),
            pltpu.VMEM((64, 128), bf16),
            *buffers,
            pltpu.SemaphoreType.DMA((3,)),
            pltpu.SemaphoreType.DMA((7,)),
            pltpu.SemaphoreType.DMA((7,)),
            pltpu.SemaphoreType.DMA((2,)),
            pltpu.SemaphoreType.DMA((2, phases)),
            pltpu.SemaphoreType.DMA((2, phases)),
        ],
        compiler_params=pltpu.CompilerParams(
            collective_id=0, has_side_effects=True, vmem_limit_bytes=60 * 2**20
        ),
    )(field, cotangent, weights)
    return grad[:, :96].reshape(field.shape), kernels.astype(f32)


def solution(mesh):
    in_specs = (P("gx", "gy", None, None), P("gx", "gy", None, None), P())
    out_specs = (P("gx", "gy", None, None), P())
    return jax.shard_map(
        on_device, mesh=mesh, in_specs=in_specs, out_specs=out_specs, check_vma=False
    )
```

```python
import functools

import jax
import jax.numpy as jnp
from jax import lax
from jax.experimental import pallas as pl
from jax.experimental.pallas import tpu as pltpu
from jax.sharding import PartitionSpec as P

MESH = pl.DeviceIdType.MESH
bf16, f32 = jnp.bfloat16, jnp.float32
dilations = (1, 2, 4, 8, 4, 2, 1)
offsets = [(i, j) for i in (-1, 0, 1) for j in (-1, 0, 1)]
around = [o for o in offsets if o != (0, 0)]
layer_rows = 480
groups = ((6, 5, 4), (3, 2, 1, 0))
group_rows = (1536, 2048)


def plan(size_x, size_y):
    if (size_x, size_y) == (16, 32):
        return [(1, 0), (1, 1), (1, 4), (0, 0), (0, 1)], [[(1, 2), (1, 3)], [(0, 2), (0, 3)]]
    return [(0, 0), (1, 0)], [[(0, 1)], [(1, 1)]]


def hosted(place, size_y):
    half = size_y // 2
    high, low, z = place[0] % 2, place[1] // half, place[0] // 2
    return place[0] // 2 * 2 + (high + z) % 2, (low + high) % 2 * half + place[1] % half


def host(block, size_y):
    half = size_y // 2
    z = block[0] // 2
    high = (block[0] % 2 + z) % 2
    return z * 2 + high, (block[1] // half + high) % 2 * half + block[1] % half


def own_index(group, place):
    index = 0
    for position, (axis, bit) in enumerate(group):
        index = index + (place[axis] // 2**bit) % 2 * 2**position
    return index


def partner(group, place, mask):
    coords = list(place)
    index = 0
    for position, (axis, bit) in enumerate(group):
        mine = (place[axis] // 2**bit) % 2
        if mask >> position & 1:
            coords[axis] = coords[axis] + (1 - 2 * mine) * 2**bit
            mine = 1 - mine
        index = index + mine * 2**position
    return tuple(coords), index


def kernel(
    size_x, size_y,
    field_any, cotangent_any, w_any, grad_ref, packed0, packed1,
    raw, w_raw, own, w_wide, near, sent, region, high1, high2, high5, high_own, acts, cols, back_home, landed_home,
    *rest,
):
    first, mids = plan(size_x, size_y)
    count1 = 2 ** len(first)
    phases = len(mids) + 2
    packed = (packed0, packed1)
    buffers, (raw_sem, near_send, near_recv, home_sem, sum_send, sum_recv, out_sem) = rest[:-7], rest[-7:]
    per_group = len(buffers) // 2
    stages, lands, gathers, parts, mid_lands = [], [], [], [], []
    for group in range(2):
        stage, land, gathered, *others = buffers[group * per_group : (group + 1) * per_group]
        stages.append(stage)
        lands.append(land)
        gathers.append(gathered)
        parts.append(others[::2])
        mid_lands.append(others[1::2])
    chunks = [rows // count1 for rows in group_rows]

    place = (lax.axis_index("gx"), lax.axis_index("gy"))
    mine = hosted(place, size_y)

    def step(at, i, j):
        return (at[0] + i + size_x) % size_x, (at[1] + j + size_y) % size_y

    def equal(a, b):
        return jnp.logical_and(a[0] == b[0], a[1] == b[1])

    def signal(device):
        pl.semaphore_signal(barrier, inc=1, device_id=device, device_id_type=MESH)

    loads = [
        pltpu.make_async_copy(field_any, raw.at[0], raw_sem.at[0]),
        pltpu.make_async_copy(cotangent_any, raw.at[1], raw_sem.at[1]),
        pltpu.make_async_copy(w_any, w_raw, raw_sem.at[2]),
    ]
    for load in loads:
        load.start()
    at_home = equal(mine, place)
    neighbours = {o: host(step(mine, *o), size_y) for o in around}
    targets = {o: host(step(place, *o), size_y) for o in offsets}
    kept = [equal(targets[o], place) for o in offsets if not o[1]]
    keeps = functools.reduce(jnp.logical_or, kept)
    barrier = pltpu.get_barrier_semaphore()
    for o in offsets:
        source = step(mine, *o)
        if o[1]:
            signal(source)
        else:
            pl.when(jnp.logical_not(equal(source, place)))(functools.partial(signal, source))

    for o in around:
        signal(neighbours[o])
    partners = 0
    for group in [first] + mids:
        for mask in range(1, 2 ** len(group)):
            signal(partner(group, place, mask)[0])
            partners += 1

    @pl.when(jnp.logical_not(at_home))
    def _():
        signal(host(place, size_y))

    for which in range(2):
        loads[which].wait()
        value = raw[which].astype(f32)
        planes = [value[:, :, z, :].reshape(64, 48) for z in range(2)]
        own[which] = jnp.concatenate(planes + [jnp.zeros((64, 32), f32)], axis=1).astype(bf16)
    pl.semaphore_wait(barrier, 8 + partners + jnp.where(keeps, 8, 9) + jnp.where(at_home, 0, 1))

    outward = sorted(around, key=lambda o: -abs(o[0]) - abs(o[1]))

    def scatter(number, source):
        for o in outward + [(0, 0)]:
            target = near.at[number, 7 - around.index(o) if o != (0, 0) else 8]
            copy = pltpu.make_async_remote_copy(
                src_ref=source,
                dst_ref=target,
                send_sem=near_send.at[number],
                recv_sem=near_recv.at[number],
                device_id=targets[o],
                device_id_type=MESH,
            )
            if o[1]:
                copy.start()
            else:
                pl.when(jnp.logical_not(equal(targets[o], place)))(copy.start)

                @pl.when(equal(targets[o], place))
                def _():
                    pltpu.make_async_copy(source, target, near_recv.at[number]).start()

    def exchange(number, source):
        for o in outward:
            pltpu.make_async_remote_copy(
                src_ref=source,
                dst_ref=near.at[number, 7 - around.index(o)],
                send_sem=near_send.at[number],
                recv_sem=near_recv.at[number],
                device_id=neighbours[o],
                device_id_type=MESH,
            ).start()

    def send(number, block):
        sent[number] = block
        exchange(number, sent.at[number])

    def arrived(number):
        landed = near.at[number, pl.ds(0, 9 if number in (0, 6) else 8)]
        pltpu.make_async_copy(landed, landed, near_recv.at[number]).wait()

    def spread_out(slot, number, own, change):
        for i, j in offsets:
            block = own if (i, j) == (0, 0) else near[number, around.index((i, j))].astype(f32)
            region[slot, 8 * (i + 1) : 8 * (i + 2), 8 * (j + 2) : 8 * (j + 3), :] = change(
                block
            ).reshape(8, 8, 128)

    def rounded(value):
        return value.astype(bf16).astype(f32)

    def silu(value):
        return rounded(value * jax.nn.sigmoid(value))

    def slope(value):
        sigma = jax.nn.sigmoid(value)
        return sigma * (1.0 + value * (1.0 - sigma))

    def box(slot, x, y, extent_x, extent_y):
        return region[slot, x : x + extent_x, y + 8 : y + 8 + extent_y, :].reshape(
            extent_x * extent_y, 128
        )

    def put(slot, x, y, extent_x, extent_y, value):
        region[slot, x : x + extent_x, y + 8 : y + 8 + extent_y, :] = value.reshape(
            extent_x, extent_y, 128
        )

    def fill(slot, spread, x, y, extent_x, extent_y):
        rows = extent_x * extent_y
        for index, (i, j) in enumerate(offsets):
            cols[:rows, index * 128 : (index + 1) * 128] = box(
                slot, x + i * spread, y + j * spread, extent_x, extent_y
            ).astype(bf16)
        return rows

    def forward(layer, rows):
        return jnp.dot(cols[:rows], w_wide[layer], preferred_element_type=f32)

    def backward(layer, rows):
        total = None
        for index in range(9):
            term = lax.dot_general(
                cols[:rows, index * 128 : (index + 1) * 128],
                w_wide[layer, index * 128 : (index + 1) * 128],
                (((1,), (1,)), ((), ())),
                preferred_element_type=f32,
            )
            total = term if total is None else total + term
        return total

    lane = lax.broadcasted_iota(jnp.int32, (48, 128), 1)

    def roll(value, left):
        return pltpu.roll(value, (128 - left) % 128, 1) if left % 128 else value

    def pack(layer):
        group = 0 if layer in groups[0] else 1
        slot, layers, stage = groups[group].index(layer), len(groups[group]), stages[group]
        turned = jnp.transpose(acts[layer].astype(f32)).astype(bf16)
        base = slot * layer_rows
        rest = None
        for index in range(9):
            shifted = cols[:64, index * 128 : (index + 1) * 128]
            piece = jnp.dot(turned, shifted, preferred_element_type=f32)
            low, high = piece[:48], piece[48:96]
            moved = roll(high, 48)
            main = low + jnp.where((lane >= 48) & (lane < 96), 0.0, moved)
            stage[base + index * 48 : base + (index + 1) * 48] = main.astype(bf16)
            tail = jnp.where(lane < 16, high, 0.0)
            if index < 8:
                tail = roll(tail, 128 - 16 * index)
                rest = tail if rest is None else rest + tail
            else:
                last = roll(tail, 128 - 16 * slot)
        stage[base + 432 : base + 480] = rest.astype(bf16)
        shared = slice(layers * layer_rows, layers * layer_rows + 48)
        if slot:
            last = last + stage[shared].astype(f32)
        stage[shared] = last.astype(bf16)

    index1 = own_index(first, place)

    def piece_of(group, index):
        return pl.ds(pl.multiple_of(index * chunks[group], chunks[group]), chunks[group])

    def copies(group, phase, members, source, target):
        for mask in reversed(range(1, 2 ** len(members))):
            device, index = partner(members, place, mask)
            pltpu.make_async_remote_copy(
                src_ref=source(index),
                dst_ref=target(mask),
                send_sem=sum_send.at[group, phase],
                recv_sem=sum_recv.at[group, phase],
                device_id=device,
                device_id_type=MESH,
            ).start()

    def received(group, phase):
        if phase == 0:
            return lands[group]
        if phase < phases - 1:
            return mid_lands[group][phase - 1]
        return gathers[group].at[pl.ds(0, (count1 - 1) * chunks[group])]

    def landed(group, phase):
        ref = received(group, phase)
        pltpu.make_async_copy(ref, ref, sum_recv.at[group, phase]).wait()

    def sum_send_first(group):
        copies(
            group, 0, first,
            lambda index: stages[group].at[piece_of(group, index)],
            lambda mask: lands[group].at[mask - 1],
        )

    def sum_step(group, phase):
        landed(group, phase)
        if phase == 0:
            terms = [stages[group][piece_of(group, index1)].astype(f32)]
            land, count = lands[group], count1
        else:
            terms = [parts[group][phase - 1][...].astype(f32)]
            land, count = mid_lands[group][phase - 1], 2 ** len(mids[phase - 1])
        terms += [land[mask - 1].astype(f32) for mask in range(1, count)]
        while len(terms) > 1:
            terms = [a + b for a, b in zip(terms[::2], terms[1::2])]
        total = terms[0].astype(bf16)
        if phase < len(mids):
            part = parts[group][phase]
            part[...] = total
            copies(
                group, phase + 1, mids[phase],
                lambda index: part,
                lambda mask: mid_lands[group][phase].at[mask - 1],
            )
        else:
            gathers[group][piece_of(group, index1)] = total
            whole = gathers[group].at[piece_of(group, index1)]
            copies(group, phase + 1, first, lambda index: whole, lambda mask: whole)

    scatter(0, own.at[0])
    region[...] = jnp.zeros_like(region)
    w_wide[...] = jnp.zeros_like(w_wide)
    for group in range(2):
        used = len(groups[group]) * layer_rows + 48
        stages[group][used:] = jnp.zeros((group_rows[group] - used, 128), bf16)
    loads[2].wait()
    zeros32 = jnp.zeros((48, 32), f32)

    def widen(layer, carry):
        for index in range(9):
            minus, same, plus = (w_raw[layer, 3 * index + k].astype(f32) for k in range(3))
            w_wide[layer, index * 128 : index * 128 + 48] = jnp.concatenate(
                [same, minus, zeros32], axis=1
            ).astype(bf16)
            w_wide[layer, index * 128 + 48 : index * 128 + 96] = jnp.concatenate(
                [plus, same, zeros32], axis=1
            ).astype(bf16)
        return carry

    lax.fori_loop(0, 7, widen, 0)

    arrived(0)
    high0 = near[0, 8].astype(f32)
    acts[0] = silu(high0).astype(bf16)
    spread_out(0, 0, high0, lambda value: value)
    spread_out(1, 0, high0, silu)
    rows = fill(1, 1, 2, 0, 20, 24)
    scatter(6, own.at[1])
    value = rounded(box(0, 2, 0, 20, 24) + forward(0, rows))
    put(0, 2, 0, 20, 24, value)
    put(1, 2, 0, 20, 24, silu(value))
    high1[...] = box(0, 7, 4, 10, 16)
    acts[1] = box(1, 8, 8, 8, 8).astype(bf16)
    rows = fill(1, 2, 4, 4, 16, 16)
    value = rounded(box(0, 4, 4, 16, 16) + forward(1, rows))
    put(0, 4, 4, 16, 16, value)
    put(1, 4, 4, 16, 16, silu(value))
    high2[...] = box(0, 5, 4, 14, 16)
    acts[2] = box(1, 8, 8, 8, 8).astype(bf16)
    rows = fill(1, 4, 8, 8, 8, 8)
    high3 = rounded(box(0, 8, 8, 8, 8) + forward(2, rows))
    high_own[0] = high3
    active = silu(high3).astype(bf16)
    acts[3] = active
    send(1, active)
    arrived(1)

    def fill_blocks(number, own):
        for index, (i, j) in enumerate(offsets):
            block = own if (i, j) == (0, 0) else near[number, around.index((i, j))]
            cols[:64, index * 128 : (index + 1) * 128] = block

    fill_blocks(1, acts[3])
    high4 = rounded(high_own[0] + forward(3, 64))
    high_own[1] = high4
    send(2, high4.astype(bf16))
    acts[4] = silu(high4).astype(bf16)
    arrived(6)
    spread_out(2, 6, near[6, 8].astype(f32), lambda value: value)
    arrived(2)
    spread_out(0, 2, high_own[1], lambda value: value)
    spread_out(1, 2, high_own[1], silu)
    rows = fill(1, 4, 4, 4, 16, 16)
    value = rounded(box(0, 4, 4, 16, 16) + forward(4, rows))
    high5[...] = value
    put(0, 4, 4, 16, 16, value)
    put(1, 4, 4, 16, 16, silu(value))
    acts[5] = box(1, 8, 8, 8, 8).astype(bf16)
    rows = fill(1, 2, 8, 8, 8, 8)
    high6 = rounded(box(0, 8, 8, 8, 8) + forward(5, rows))
    high_own[2] = high6
    acts[6] = silu(high6).astype(bf16)

    def fill_back(slot, spread, x, y, extent_x, extent_y):
        return fill(slot, -spread, x, y, extent_x, extent_y)

    rows = fill_back(2, 1, 8, 8, 8, 8)
    grad6 = (near[6, 8].astype(f32) + slope(high_own[2]) * backward(6, rows)).astype(bf16)
    send(3, grad6)
    pack(6)
    arrived(3)
    spread_out(2, 3, sent[3].astype(f32), lambda value: value)
    rows = fill_back(2, 2, 4, 4, 16, 16)
    value = rounded(box(2, 4, 4, 16, 16) + slope(high5[...]) * backward(5, rows))
    put(0, 4, 4, 16, 16, value)
    rows = fill_back(0, 4, 8, 8, 8, 8)
    grad4 = (box(0, 8, 8, 8, 8) + slope(high_own[1]) * backward(4, rows)).astype(bf16)
    send(4, grad4)
    pack(4)
    fill_back(2, 2, 8, 8, 8, 8)
    pack(5)
    sum_send_first(0)
    arrived(4)

    def fill_blocks_back(number, own):
        for index, (i, j) in enumerate(offsets):
            block = own if (i, j) == (0, 0) else near[number, around.index((-i, -j))]
            cols[:64, index * 128 : (index + 1) * 128] = block

    fill_blocks_back(4, sent[4])
    grad3 = (sent[4].astype(f32) + slope(high_own[0]) * backward(3, 64)).astype(bf16)
    send(5, grad3)
    pack(3)
    sum_step(0, 0)
    arrived(5)
    spread_out(2, 5, sent[5].astype(f32), lambda value: value)
    rows = fill_back(2, 4, 5, 4, 14, 16)
    value = rounded(box(2, 5, 4, 14, 16) + slope(high2[...]) * backward(2, rows))
    put(0, 5, 4, 14, 16, value)
    fill_back(2, 4, 8, 8, 8, 8)
    pack(2)
    rows = fill_back(0, 2, 7, 4, 10, 16)
    value = rounded(box(0, 7, 4, 10, 16) + slope(high1[...]) * backward(1, rows))
    put(1, 7, 4, 10, 16, value)
    fill_back(0, 2, 8, 8, 8, 8)
    pack(1)
    sum_step(0, 1)
    rows = fill_back(1, 1, 8, 8, 8, 8)
    pack(0)
    sum_send_first(1)
    back_home[...] = (
        box(1, 8, 8, 8, 8) + slope(near[0, 8].astype(f32)) * backward(0, rows)
    ).astype(bf16)
    to_owner = pltpu.make_async_remote_copy(
        src_ref=back_home,
        dst_ref=landed_home,
        send_sem=home_sem.at[0],
        recv_sem=home_sem.at[1],
        device_id=mine,
        device_id_type=MESH,
    )

    @pl.when(jnp.logical_not(at_home))
    def _():
        to_owner.start()

    @pl.when(at_home)
    def _():
        landed_home[...] = back_home[...]

    sum_step(1, 0)
    sum_step(0, 2)
    for phase in range(1, phases - 1):
        sum_step(1, phase)

    @pl.when(jnp.logical_not(at_home))
    def _():
        to_owner.wait()

    grad_ref[...] = landed_home[...]
    for number in range(1, 6):
        ref = near.at[number, pl.ds(0, 8)]
        pltpu.make_async_copy(ref, ref, near_send.at[number]).wait()
    for number in (0, 6):
        for count, chosen in ((8, keeps), (9, jnp.logical_not(keeps))):

            @pl.when(chosen)
            def _():
                ref = near.at[number, pl.ds(0, count)]
                pltpu.make_async_copy(ref, ref, near_send.at[number]).wait()

    stores = []
    for group in range(2):
        landed(group, phases - 1)
        stores.append(pltpu.make_async_copy(gathers[group], packed[group], out_sem.at[group]))
        stores[group].start()
    for group in range(2):
        for phase in range(phases):
            ref = received(group, phase)
            pltpu.make_async_copy(ref, ref, sum_send.at[group, phase]).wait()
    for store in stores:
        store.wait()


def unpack(packed0, packed1, block_ref, field_ref, out_any, held0, held1, wide, in_sem, out_sem):
    loads = [
        pltpu.make_async_copy(packed, held, in_sem.at[group])
        for group, (packed, held) in enumerate(((packed0, held0), (packed1, held1)))
    ]
    for load in loads:
        load.start()
    block = block_ref[...].astype(f32).reshape(8, 8, 128)
    field_ref[...] = jnp.stack([block[:, :, :48], block[:, :, 48:96]], axis=2).astype(bf16)
    lane = lax.broadcasted_iota(jnp.int32, (48, 128), 1)

    def roll(value, left):
        return pltpu.roll(value, (128 - left) % 128, 1) if left % 128 else value

    stores = []
    for group, held in enumerate((held0, held1)):
        loads[group].wait()
        shared = len(groups[group]) * layer_rows
        shared = held[shared : shared + 48].astype(f32)
        for slot, layer in enumerate(groups[group]):
            base = slot * layer_rows
            rest = held[base + 432 : base + 480].astype(f32)
            for index in range(9):
                main = held[base + index * 48 : base + (index + 1) * 48].astype(f32)
                tail = roll(rest, 16 * index) if index < 8 else roll(shared, 16 * slot)
                plus = jnp.where(lane < 16, tail, roll(main, 80))
                for k, value in enumerate((roll(main, 48), main, plus)):
                    wide[layer, 3 * index + k] = value[:, :48]
            stores.append(pltpu.make_async_copy(wide.at[layer], out_any.at[layer], out_sem.at[layer]))
            stores[-1].start()
    for store in stores:
        store.wait()


def on_device(field, cotangent, weights):
    size_x, size_y = lax.axis_size("gx"), lax.axis_size("gy")
    first, mids = plan(size_x, size_y)
    count1 = 2 ** len(first)
    vmem = pl.BlockSpec(memory_space=pltpu.VMEM)
    far = pl.BlockSpec(memory_space=pl.ANY)
    buffers = []
    for rows in group_rows:
        chunk = rows // count1
        buffers += [
            pltpu.VMEM((rows, 128), bf16),
            pltpu.VMEM((count1 - 1, chunk, 128), bf16),
            pltpu.VMEM((rows, 128), bf16),
        ]
        for members in mids:
            buffers += [
                pltpu.VMEM((chunk, 128), bf16),
                pltpu.VMEM((2 ** len(members) - 1, chunk, 128), bf16),
            ]
    phases = len(mids) + 2
    grad, *sums = pl.pallas_call(
        functools.partial(kernel, size_x, size_y),
        out_shape=(
            jax.ShapeDtypeStruct((64, 128), bf16),
            *[jax.ShapeDtypeStruct((rows, 128), bf16) for rows in group_rows],
        ),
        in_specs=[far] * 3,
        out_specs=(vmem, far, far),
        scratch_shapes=[
            pltpu.VMEM((2,) + field.shape, bf16),
            pltpu.VMEM(weights.shape, bf16),
            pltpu.VMEM((2, 64, 128), bf16),
            pltpu.VMEM((7, 1152, 128), bf16),
            pltpu.VMEM((7, 9, 64, 128), bf16),
            pltpu.VMEM((6, 64, 128), bf16),
            pltpu.VMEM((3, 24, 40, 128), f32),
            pltpu.VMEM((160, 128), f32),
            pltpu.VMEM((224, 128), f32),
            pltpu.VMEM((256, 128), f32),
            pltpu.VMEM((3, 64, 128), f32),
            pltpu.VMEM((7, 64, 128), bf16),
            pltpu.VMEM((480, 1152), bf16),
            pltpu.VMEM((64, 128), bf16),
            pltpu.VMEM((64, 128), bf16),
            *buffers,
            pltpu.SemaphoreType.DMA((3,)),
            pltpu.SemaphoreType.DMA((7,)),
            pltpu.SemaphoreType.DMA((7,)),
            pltpu.SemaphoreType.DMA((2,)),
            pltpu.SemaphoreType.DMA((2, phases)),
            pltpu.SemaphoreType.DMA((2, phases)),
            pltpu.SemaphoreType.DMA((2,)),
        ],
        compiler_params=pltpu.CompilerParams(
            collective_id=0, has_side_effects=True, vmem_limit_bytes=60 * 2**20
        ),
    )(field, cotangent, weights)
    return pl.pallas_call(
        unpack,
        out_shape=(
            jax.ShapeDtypeStruct(field.shape, bf16),
            jax.ShapeDtypeStruct(weights.shape, f32),
        ),
        in_specs=[far, far, vmem],
        out_specs=(vmem, far),
        scratch_shapes=[
            *[pltpu.VMEM((rows, 128), bf16) for rows in group_rows],
            pltpu.VMEM(weights.shape, f32),
            pltpu.SemaphoreType.DMA((2,)),
            pltpu.SemaphoreType.DMA((7,)),
        ],
        compiler_params=pltpu.CompilerParams(vmem_limit_bytes=60 * 2**20),
    )(*sums, grad)


def solution(mesh):
    in_specs = (P("gx", "gy", None, None), P("gx", "gy", None, None), P())
    out_specs = (P("gx", "gy", None, None), P())
    return jax.shard_map(
        on_device, mesh=mesh, in_specs=in_specs, out_specs=out_specs, check_vma=False
    )
```

```python
import functools

import jax
import jax.numpy as jnp
from jax import lax
from jax.experimental import pallas as pl
from jax.experimental.pallas import tpu as pltpu
from jax.sharding import PartitionSpec as P

MESH = pl.DeviceIdType.MESH
bf16, f32 = jnp.bfloat16, jnp.float32
dilations = (1, 2, 4, 8, 4, 2, 1)
offsets = [(i, j) for i in (-1, 0, 1) for j in (-1, 0, 1)]
around = [o for o in offsets if o != (0, 0)]
layer_rows = 480
groups = ((6, 5, 4), (3, 2, 1, 0))
group_rows = (1536, 2048)


def plan(size_x, size_y):
    if (size_x, size_y) == (16, 32):
        return [(1, 0), (1, 1), (1, 4), (0, 0), (0, 1)], [[(1, 2), (1, 3)], [(0, 2), (0, 3)]]
    return [(0, 0), (1, 0)], [[(0, 1)], [(1, 1)]]


def hosted(place, size_y):
    half = size_y // 2
    high, low, z = place[0] % 2, place[1] // half, place[0] // 2
    return place[0] // 2 * 2 + (high + z) % 2, (low + high) % 2 * half + place[1] % half


def host(block, size_y):
    half = size_y // 2
    z = block[0] // 2
    high = (block[0] % 2 + z) % 2
    return z * 2 + high, (block[1] // half + high) % 2 * half + block[1] % half


def own_index(group, place):
    index = 0
    for position, (axis, bit) in enumerate(group):
        index = index + (place[axis] // 2**bit) % 2 * 2**position
    return index


def partner(group, place, mask):
    coords = list(place)
    index = 0
    for position, (axis, bit) in enumerate(group):
        mine = (place[axis] // 2**bit) % 2
        if mask >> position & 1:
            coords[axis] = coords[axis] + (1 - 2 * mine) * 2**bit
            mine = 1 - mine
        index = index + mine * 2**position
    return tuple(coords), index


def kernel(
    size_x, size_y,
    field_any, cotangent_any, w_any, grad_any, packed0, packed1,
    raw, w_raw, own, w_wide, w_side, near, sent, region, high1, high2, high5, high_own, acts, cols, back_home, landed_home,
    *rest,
):
    first, mids = plan(size_x, size_y)
    count1 = 2 ** len(first)
    phases = len(mids) + 2
    packed = (packed0, packed1)
    buffers, (raw_sem, near_send, near_recv, home_sem, sum_send, sum_recv, out_sem) = rest[:-7], rest[-7:]
    per_group = len(buffers) // 2
    stages, lands, gathers, parts, mid_lands = [], [], [], [], []
    for group in range(2):
        stage, land, gathered, *others = buffers[group * per_group : (group + 1) * per_group]
        stages.append(stage)
        lands.append(land)
        gathers.append(gathered)
        parts.append(others[::2])
        mid_lands.append(others[1::2])
    chunks = [rows // count1 for rows in group_rows]

    place = (lax.axis_index("gx"), lax.axis_index("gy"))
    mine = hosted(place, size_y)

    def step(at, i, j):
        return (at[0] + i + size_x) % size_x, (at[1] + j + size_y) % size_y

    def equal(a, b):
        return jnp.logical_and(a[0] == b[0], a[1] == b[1])

    def signal(device):
        pl.semaphore_signal(barrier, inc=1, device_id=device, device_id_type=MESH)

    loads = [
        pltpu.make_async_copy(field_any, raw.at[0], raw_sem.at[0]),
        pltpu.make_async_copy(cotangent_any, raw.at[1], raw_sem.at[1]),
        pltpu.make_async_copy(w_any, w_raw, raw_sem.at[2]),
    ]
    for load in loads:
        load.start()
    at_home = equal(mine, place)
    neighbours = {o: host(step(mine, *o), size_y) for o in around}
    targets = {o: host(step(place, *o), size_y) for o in offsets}
    kept = [equal(targets[o], place) for o in offsets if not o[1]]
    keeps = functools.reduce(jnp.logical_or, kept)
    barrier = pltpu.get_barrier_semaphore()
    for o in offsets:
        source = step(mine, *o)
        if o[1]:
            signal(source)
        else:
            pl.when(jnp.logical_not(equal(source, place)))(functools.partial(signal, source))

    for o in around:
        signal(neighbours[o])
    partners = 0
    for group in [first] + mids:
        for mask in range(1, 2 ** len(group)):
            signal(partner(group, place, mask)[0])
            partners += 1

    @pl.when(jnp.logical_not(at_home))
    def _():
        signal(host(place, size_y))


    def lay_out(which):
        loads[which].wait()
        value = raw[which].astype(f32)
        planes = [value[:, :, z, :].reshape(64, 48) for z in range(2)]
        own[which] = jnp.concatenate(planes + [jnp.zeros((64, 32), f32)], axis=1).astype(bf16)

    lay_out(0)
    pl.semaphore_wait(barrier, 8 + partners + jnp.where(keeps, 8, 9) + jnp.where(at_home, 0, 1))

    outward = sorted(around, key=lambda o: -abs(o[0]) - abs(o[1]))

    def scatter(number, source):
        for o in outward + [(0, 0)]:
            target = near.at[number, 7 - around.index(o) if o != (0, 0) else 8]
            copy = pltpu.make_async_remote_copy(
                src_ref=source,
                dst_ref=target,
                send_sem=near_send.at[number],
                recv_sem=near_recv.at[number],
                device_id=targets[o],
                device_id_type=MESH,
            )
            if o[1]:
                copy.start()
            else:
                pl.when(jnp.logical_not(equal(targets[o], place)))(copy.start)

                @pl.when(equal(targets[o], place))
                def _():
                    pltpu.make_async_copy(source, target, near_recv.at[number]).start()

    def exchange(number, source):
        for o in outward:
            pltpu.make_async_remote_copy(
                src_ref=source,
                dst_ref=near.at[number, 7 - around.index(o)],
                send_sem=near_send.at[number],
                recv_sem=near_recv.at[number],
                device_id=neighbours[o],
                device_id_type=MESH,
            ).start()

    def send(number, block):
        sent[number] = block
        exchange(number, sent.at[number])

    def arrived(number):
        landed = near.at[number, pl.ds(0, 9 if number in (0, 6) else 8)]
        pltpu.make_async_copy(landed, landed, near_recv.at[number]).wait()

    def spread_out(slot, number, own, change):
        for i, j in offsets:
            block = own if (i, j) == (0, 0) else near[number, around.index((i, j))].astype(f32)
            region[slot, 8 * (i + 1) : 8 * (i + 2), 8 * (j + 2) : 8 * (j + 3), :] = change(
                block
            ).reshape(8, 8, 128)

    def rounded(value):
        return value.astype(bf16).astype(f32)

    def silu(value):
        return rounded(value * jax.nn.sigmoid(value))

    def slope(value):
        sigma = jax.nn.sigmoid(value)
        return sigma * (1.0 + value * (1.0 - sigma))

    def box(slot, x, y, extent_x, extent_y):
        return region[slot, x : x + extent_x, y + 8 : y + 8 + extent_y, :].reshape(
            extent_x * extent_y, 128
        )

    def put(slot, x, y, extent_x, extent_y, value):
        region[slot, x : x + extent_x, y + 8 : y + 8 + extent_y, :] = value.reshape(
            extent_x, extent_y, 128
        )

    def fill(slot, spread, x, y, extent_x, extent_y):
        rows = extent_x * extent_y
        for index, (i, j) in enumerate(offsets):
            cols[:rows, index * 128 : (index + 1) * 128] = box(
                slot, x + i * spread, y + j * spread, extent_x, extent_y
            ).astype(bf16)
        return rows

    def forward(layer, rows):
        return jnp.dot(cols[:rows], w_wide[layer], preferred_element_type=f32)

    def backward(layer, rows):
        return lax.dot_general(
            cols[:rows], w_side[layer], (((1,), (1,)), ((), ())), preferred_element_type=f32
        )

    lane = lax.broadcasted_iota(jnp.int32, (48, 128), 1)

    def roll(value, left):
        return pltpu.roll(value, (128 - left) % 128, 1) if left % 128 else value

    def pack(layer):
        group = 0 if layer in groups[0] else 1
        slot, layers, stage = groups[group].index(layer), len(groups[group]), stages[group]
        turned = jnp.transpose(acts[layer].astype(f32)).astype(bf16)
        base = slot * layer_rows
        rest = None
        for index in range(9):
            shifted = cols[:64, index * 128 : (index + 1) * 128]
            piece = jnp.dot(turned, shifted, preferred_element_type=f32)
            low, high = piece[:48], piece[48:96]
            moved = roll(high, 48)
            main = low + jnp.where((lane >= 48) & (lane < 96), 0.0, moved)
            stage[base + index * 48 : base + (index + 1) * 48] = main.astype(bf16)
            tail = jnp.where(lane < 16, high, 0.0)
            if index < 8:
                tail = roll(tail, 128 - 16 * index)
                rest = tail if rest is None else rest + tail
            else:
                last = roll(tail, 128 - 16 * slot)
        stage[base + 432 : base + 480] = rest.astype(bf16)
        shared = slice(layers * layer_rows, layers * layer_rows + 48)
        if slot:
            last = last + stage[shared].astype(f32)
        stage[shared] = last.astype(bf16)

    index1 = own_index(first, place)

    def piece_of(group, index):
        return pl.ds(pl.multiple_of(index * chunks[group], chunks[group]), chunks[group])

    def copies(group, phase, members, source, target):
        for mask in reversed(range(1, 2 ** len(members))):
            device, index = partner(members, place, mask)
            pltpu.make_async_remote_copy(
                src_ref=source(index),
                dst_ref=target(mask),
                send_sem=sum_send.at[group, phase],
                recv_sem=sum_recv.at[group, phase],
                device_id=device,
                device_id_type=MESH,
            ).start()

    def received(group, phase):
        if phase == 0:
            return lands[group]
        if phase < phases - 1:
            return mid_lands[group][phase - 1]
        return gathers[group].at[pl.ds(0, (count1 - 1) * chunks[group])]

    def landed(group, phase):
        ref = received(group, phase)
        pltpu.make_async_copy(ref, ref, sum_recv.at[group, phase]).wait()

    def sum_send_first(group):
        copies(
            group, 0, first,
            lambda index: stages[group].at[piece_of(group, index)],
            lambda mask: lands[group].at[mask - 1],
        )

    def sum_step(group, phase):
        landed(group, phase)
        if phase == 0:
            terms = [stages[group][piece_of(group, index1)].astype(f32)]
            land, count = lands[group], count1
        else:
            terms = [parts[group][phase - 1][...].astype(f32)]
            land, count = mid_lands[group][phase - 1], 2 ** len(mids[phase - 1])
        terms += [land[mask - 1].astype(f32) for mask in range(1, count)]
        while len(terms) > 1:
            terms = [a + b for a, b in zip(terms[::2], terms[1::2])]
        total = terms[0].astype(bf16)
        if phase < len(mids):
            part = parts[group][phase]
            part[...] = total
            copies(
                group, phase + 1, mids[phase],
                lambda index: part,
                lambda mask: mid_lands[group][phase].at[mask - 1],
            )
        else:
            gathers[group][piece_of(group, index1)] = total
            whole = gathers[group].at[piece_of(group, index1)]
            copies(group, phase + 1, first, lambda index: whole, lambda mask: whole)

    scatter(0, own.at[0])
    lay_out(1)
    region[...] = jnp.zeros_like(region)
    w_wide[...] = jnp.zeros_like(w_wide)
    w_side[:, 96:] = jnp.zeros((7, 32, 1152), bf16)
    for group in range(2):
        used = len(groups[group]) * layer_rows + 48
        stages[group][used:] = jnp.zeros((group_rows[group] - used, 128), bf16)
    loads[2].wait()
    zeros32 = jnp.zeros((48, 32), f32)

    def widen(layer, carry):
        for index in range(9):
            minus, same, plus = (w_raw[layer, 3 * index + k].astype(f32) for k in range(3))
            low = jnp.concatenate([same, minus, zeros32], axis=1).astype(bf16)
            high = jnp.concatenate([plus, same, zeros32], axis=1).astype(bf16)
            w_wide[layer, index * 128 : index * 128 + 48] = low
            w_wide[layer, index * 128 + 48 : index * 128 + 96] = high
            w_side[layer, :48, index * 128 : (index + 1) * 128] = low
            w_side[layer, 48:96, index * 128 : (index + 1) * 128] = high
        return carry

    lax.fori_loop(0, 7, widen, 0)

    arrived(0)
    high0 = near[0, 8].astype(f32)
    acts[0] = silu(high0).astype(bf16)
    spread_out(0, 0, high0, lambda value: value)
    spread_out(1, 0, high0, silu)
    rows = fill(1, 1, 2, 0, 20, 24)
    scatter(6, own.at[1])
    value = rounded(box(0, 2, 0, 20, 24) + forward(0, rows))
    put(0, 2, 0, 20, 24, value)
    put(1, 2, 0, 20, 24, silu(value))
    high1[...] = box(0, 7, 4, 10, 16)
    acts[1] = box(1, 8, 8, 8, 8).astype(bf16)
    rows = fill(1, 2, 4, 4, 16, 16)
    value = rounded(box(0, 4, 4, 16, 16) + forward(1, rows))
    put(0, 4, 4, 16, 16, value)
    put(1, 4, 4, 16, 16, silu(value))
    high2[...] = box(0, 5, 4, 14, 16)
    acts[2] = box(1, 8, 8, 8, 8).astype(bf16)
    rows = fill(1, 4, 8, 8, 8, 8)
    high3 = rounded(box(0, 8, 8, 8, 8) + forward(2, rows))
    high_own[0] = high3
    active = silu(high3).astype(bf16)
    acts[3] = active
    send(1, active)
    arrived(1)

    def fill_blocks(number, own):
        for index, (i, j) in enumerate(offsets):
            block = own if (i, j) == (0, 0) else near[number, around.index((i, j))]
            cols[:64, index * 128 : (index + 1) * 128] = block

    fill_blocks(1, acts[3])
    high4 = rounded(high_own[0] + forward(3, 64))
    high_own[1] = high4
    send(2, high4.astype(bf16))
    acts[4] = silu(high4).astype(bf16)
    arrived(6)
    spread_out(2, 6, near[6, 8].astype(f32), lambda value: value)
    arrived(2)
    spread_out(0, 2, high_own[1], lambda value: value)
    spread_out(1, 2, high_own[1], silu)
    rows = fill(1, 4, 4, 4, 16, 16)
    value = rounded(box(0, 4, 4, 16, 16) + forward(4, rows))
    high5[...] = value
    put(0, 4, 4, 16, 16, value)
    put(1, 4, 4, 16, 16, silu(value))
    acts[5] = box(1, 8, 8, 8, 8).astype(bf16)
    rows = fill(1, 2, 8, 8, 8, 8)
    high6 = rounded(box(0, 8, 8, 8, 8) + forward(5, rows))
    high_own[2] = high6
    acts[6] = silu(high6).astype(bf16)

    def fill_back(slot, spread, x, y, extent_x, extent_y):
        return fill(slot, -spread, x, y, extent_x, extent_y)

    rows = fill_back(2, 1, 8, 8, 8, 8)
    grad6 = (near[6, 8].astype(f32) + slope(high_own[2]) * backward(6, rows)).astype(bf16)
    send(3, grad6)
    pack(6)
    arrived(3)
    spread_out(2, 3, sent[3].astype(f32), lambda value: value)
    rows = fill_back(2, 2, 4, 4, 16, 16)
    value = rounded(box(2, 4, 4, 16, 16) + slope(high5[...]) * backward(5, rows))
    put(0, 4, 4, 16, 16, value)
    rows = fill_back(0, 4, 8, 8, 8, 8)
    grad4 = (box(0, 8, 8, 8, 8) + slope(high_own[1]) * backward(4, rows)).astype(bf16)
    send(4, grad4)
    pack(4)
    fill_back(2, 2, 8, 8, 8, 8)
    pack(5)
    sum_send_first(0)
    arrived(4)

    def fill_blocks_back(number, own):
        for index, (i, j) in enumerate(offsets):
            block = own if (i, j) == (0, 0) else near[number, around.index((-i, -j))]
            cols[:64, index * 128 : (index + 1) * 128] = block

    fill_blocks_back(4, sent[4])
    grad3 = (sent[4].astype(f32) + slope(high_own[0]) * backward(3, 64)).astype(bf16)
    send(5, grad3)
    pack(3)
    sum_step(0, 0)
    arrived(5)
    spread_out(2, 5, sent[5].astype(f32), lambda value: value)
    rows = fill_back(2, 4, 5, 4, 14, 16)
    value = rounded(box(2, 5, 4, 14, 16) + slope(high2[...]) * backward(2, rows))
    put(0, 5, 4, 14, 16, value)
    fill_back(2, 4, 8, 8, 8, 8)
    pack(2)
    rows = fill_back(0, 2, 7, 4, 10, 16)
    value = rounded(box(0, 7, 4, 10, 16) + slope(high1[...]) * backward(1, rows))
    put(1, 7, 4, 10, 16, value)
    fill_back(0, 2, 8, 8, 8, 8)
    pack(1)
    sum_step(0, 1)
    rows = fill_back(1, 1, 8, 8, 8, 8)
    pack(0)
    sum_send_first(1)
    back_home[...] = (
        box(1, 8, 8, 8, 8) + slope(near[0, 8].astype(f32)) * backward(0, rows)
    ).astype(bf16)
    to_owner = pltpu.make_async_remote_copy(
        src_ref=back_home,
        dst_ref=landed_home,
        send_sem=home_sem.at[0],
        recv_sem=home_sem.at[1],
        device_id=mine,
        device_id_type=MESH,
    )

    @pl.when(jnp.logical_not(at_home))
    def _():
        to_owner.start()

    @pl.when(at_home)
    def _():
        landed_home[...] = back_home[...]

    sum_step(1, 0)
    sum_step(0, 2)
    for phase in range(1, phases - 1):
        sum_step(1, phase)

    @pl.when(jnp.logical_not(at_home))
    def _():
        to_owner.wait()

    grad_store = pltpu.make_async_copy(landed_home, grad_any, raw_sem.at[0])
    grad_store.start()
    for number in range(1, 6):
        ref = near.at[number, pl.ds(0, 8)]
        pltpu.make_async_copy(ref, ref, near_send.at[number]).wait()
    for number in (0, 6):
        for count, chosen in ((8, keeps), (9, jnp.logical_not(keeps))):

            @pl.when(chosen)
            def _():
                ref = near.at[number, pl.ds(0, count)]
                pltpu.make_async_copy(ref, ref, near_send.at[number]).wait()

    stores = []
    for group in range(2):
        landed(group, phases - 1)
        stores.append(pltpu.make_async_copy(gathers[group], packed[group], out_sem.at[group]))
        stores[group].start()
    for group in range(2):
        for phase in range(phases):
            ref = received(group, phase)
            pltpu.make_async_copy(ref, ref, sum_send.at[group, phase]).wait()
    for store in stores:
        store.wait()
    grad_store.wait()


def unpack(packed0, packed1, block_any, field_any, out_any, held0, held1, block, cells, wide, in_sem, out_sem):
    loads = [
        pltpu.make_async_copy(packed, held, in_sem.at[group])
        for group, (packed, held) in enumerate(((packed0, held0), (packed1, held1), (block_any, block)))
    ]
    for load in loads:
        load.start()
    loads[2].wait()
    rows = block[...].astype(f32).reshape(8, 8, 128)
    cells[...] = jnp.stack([rows[:, :, :48], rows[:, :, 48:96]], axis=2).astype(bf16)
    stores = [pltpu.make_async_copy(cells, field_any, out_sem.at[7])]
    stores[0].start()
    lane = lax.broadcasted_iota(jnp.int32, (48, 128), 1)

    def roll(value, left):
        return pltpu.roll(value, (128 - left) % 128, 1) if left % 128 else value

    for group, held in enumerate((held0, held1)):
        loads[group].wait()
        shared = len(groups[group]) * layer_rows
        shared = held[shared : shared + 48].astype(f32)
        for slot, layer in enumerate(groups[group]):
            base = slot * layer_rows
            rest = held[base + 432 : base + 480].astype(f32)
            for index in range(9):
                main = held[base + index * 48 : base + (index + 1) * 48].astype(f32)
                tail = roll(rest, 16 * index) if index < 8 else roll(shared, 16 * slot)
                plus = jnp.where(lane < 16, tail, roll(main, 80))
                for k, value in enumerate((roll(main, 48), main, plus)):
                    wide[layer, 3 * index + k] = value[:, :48]
            stores.append(pltpu.make_async_copy(wide.at[layer], out_any.at[layer], out_sem.at[layer]))
            stores[-1].start()
    for store in stores:
        store.wait()


def on_device(field, cotangent, weights):
    size_x, size_y = lax.axis_size("gx"), lax.axis_size("gy")
    first, mids = plan(size_x, size_y)
    count1 = 2 ** len(first)
    far = pl.BlockSpec(memory_space=pl.ANY)
    buffers = []
    for rows in group_rows:
        chunk = rows // count1
        buffers += [
            pltpu.VMEM((rows, 128), bf16),
            pltpu.VMEM((count1 - 1, chunk, 128), bf16),
            pltpu.VMEM((rows, 128), bf16),
        ]
        for members in mids:
            buffers += [
                pltpu.VMEM((chunk, 128), bf16),
                pltpu.VMEM((2 ** len(members) - 1, chunk, 128), bf16),
            ]
    phases = len(mids) + 2
    grad, *sums = pl.pallas_call(
        functools.partial(kernel, size_x, size_y),
        out_shape=(
            jax.ShapeDtypeStruct((64, 128), bf16),
            *[jax.ShapeDtypeStruct((rows, 128), bf16) for rows in group_rows],
        ),
        in_specs=[far] * 3,
        out_specs=(far, far, far),
        scratch_shapes=[
            pltpu.VMEM((2,) + field.shape, bf16),
            pltpu.VMEM(weights.shape, bf16),
            pltpu.VMEM((2, 64, 128), bf16),
            pltpu.VMEM((7, 1152, 128), bf16),
            pltpu.VMEM((7, 128, 1152), bf16),
            pltpu.VMEM((7, 9, 64, 128), bf16),
            pltpu.VMEM((6, 64, 128), bf16),
            pltpu.VMEM((3, 24, 40, 128), f32),
            pltpu.VMEM((160, 128), f32),
            pltpu.VMEM((224, 128), f32),
            pltpu.VMEM((256, 128), f32),
            pltpu.VMEM((3, 64, 128), f32),
            pltpu.VMEM((7, 64, 128), bf16),
            pltpu.VMEM((480, 1152), bf16),
            pltpu.VMEM((64, 128), bf16),
            pltpu.VMEM((64, 128), bf16),
            *buffers,
            pltpu.SemaphoreType.DMA((3,)),
            pltpu.SemaphoreType.DMA((7,)),
            pltpu.SemaphoreType.DMA((7,)),
            pltpu.SemaphoreType.DMA((2,)),
            pltpu.SemaphoreType.DMA((2, phases)),
            pltpu.SemaphoreType.DMA((2, phases)),
            pltpu.SemaphoreType.DMA((2,)),
        ],
        compiler_params=pltpu.CompilerParams(
            collective_id=0, has_side_effects=True, vmem_limit_bytes=60 * 2**20
        ),
    )(field, cotangent, weights)
    return pl.pallas_call(
        unpack,
        out_shape=(
            jax.ShapeDtypeStruct(field.shape, bf16),
            jax.ShapeDtypeStruct(weights.shape, f32),
        ),
        in_specs=[far] * 3,
        out_specs=(far, far),
        scratch_shapes=[
            *[pltpu.VMEM((rows, 128), bf16) for rows in group_rows],
            pltpu.VMEM((64, 128), bf16),
            pltpu.VMEM(field.shape, bf16),
            pltpu.VMEM(weights.shape, f32),
            pltpu.SemaphoreType.DMA((3,)),
            pltpu.SemaphoreType.DMA((8,)),
        ],
        compiler_params=pltpu.CompilerParams(vmem_limit_bytes=60 * 2**20),
    )(*sums, grad)


def solution(mesh):
    in_specs = (P("gx", "gy", None, None), P("gx", "gy", None, None), P())
    out_specs = (P("gx", "gy", None, None), P())
    return jax.shard_map(
        on_device, mesh=mesh, in_specs=in_specs, out_specs=out_specs, check_vma=False
    )
```

```python
import functools

import jax
import jax.numpy as jnp
from jax import lax
from jax.experimental import pallas as pl
from jax.experimental.pallas import tpu as pltpu
from jax.sharding import PartitionSpec as P

MESH = pl.DeviceIdType.MESH
bf16, f32 = jnp.bfloat16, jnp.float32
dilations = (1, 2, 4, 8, 4, 2, 1)
offsets = [(i, j) for i in (-1, 0, 1) for j in (-1, 0, 1)]
around = [o for o in offsets if o != (0, 0)]
layer_rows = 480
groups = ((6, 5, 4), (3, 2, 1, 0))
group_rows = (1536, 2048)


def plan(size_x, size_y):
    if (size_x, size_y) == (16, 32):
        return [(1, 0), (1, 1), (1, 4), (0, 0), (0, 1)], [[(1, 2), (1, 3)], [(0, 2), (0, 3)]]
    return [(0, 0), (1, 0)], [[(0, 1)], [(1, 1)]]


def hosted(place, size_y):
    half = size_y // 2
    high, low, z = place[0] % 2, place[1] // half, place[0] // 2
    return place[0] // 2 * 2 + (high + z) % 2, (low + high) % 2 * half + place[1] % half


def host(block, size_y):
    half = size_y // 2
    z = block[0] // 2
    high = (block[0] % 2 + z) % 2
    return z * 2 + high, (block[1] // half + high) % 2 * half + block[1] % half


def own_index(group, place):
    index = 0
    for position, (axis, bit) in enumerate(group):
        index = index + (place[axis] // 2**bit) % 2 * 2**position
    return index


def partner(group, place, mask):
    coords = list(place)
    index = 0
    for position, (axis, bit) in enumerate(group):
        mine = (place[axis] // 2**bit) % 2
        if mask >> position & 1:
            coords[axis] = coords[axis] + (1 - 2 * mine) * 2**bit
            mine = 1 - mine
        index = index + mine * 2**position
    return tuple(coords), index


def kernel(
    size_x, size_y,
    field_any, cotangent_any, w_any, grad_any, packed0, packed1,
    raw, w_raw, own, w_wide, w_side, near, sent, region, high1, high2, high5, high_own, acts, turned, cols, back_home, landed_home,
    *rest,
):
    first, mids = plan(size_x, size_y)
    count1 = 2 ** len(first)
    phases = len(mids) + 2
    buffers, (raw_sem, near_send, near_recv, home_sem, sum_send, sum_recv, out_sem) = rest[:-7], rest[-7:]
    per_group = len(buffers) // 2
    stages, lands, gathers, parts, mid_lands = [], [], [], [], []
    for group in range(2):
        stage, land, gathered, *others = buffers[group * per_group : (group + 1) * per_group]
        stages.append(stage)
        lands.append(land)
        gathers.append(gathered)
        parts.append(others[::2])
        mid_lands.append(others[1::2])
    chunks = [rows // count1 for rows in group_rows]

    place = (lax.axis_index("gx"), lax.axis_index("gy"))
    mine = hosted(place, size_y)

    def step(at, i, j):
        return (at[0] + i + size_x) % size_x, (at[1] + j + size_y) % size_y

    def equal(a, b):
        return jnp.logical_and(a[0] == b[0], a[1] == b[1])

    def signal(device):
        pl.semaphore_signal(barrier, inc=1, device_id=device, device_id_type=MESH)

    loads = [
        pltpu.make_async_copy(field_any, raw.at[0], raw_sem.at[0]),
        pltpu.make_async_copy(cotangent_any, raw.at[1], raw_sem.at[1]),
        pltpu.make_async_copy(w_any, w_raw, raw_sem.at[2]),
    ]
    for load in loads:
        load.start()
    at_home = equal(mine, place)
    neighbours = {o: host(step(mine, *o), size_y) for o in around}
    targets = {o: host(step(place, *o), size_y) for o in offsets}
    kept = [equal(targets[o], place) for o in offsets if not o[1]]
    keeps = functools.reduce(jnp.logical_or, kept)
    barrier = pltpu.get_barrier_semaphore()
    for o in offsets:
        source = step(mine, *o)
        if o[1]:
            signal(source)
        else:
            pl.when(jnp.logical_not(equal(source, place)))(functools.partial(signal, source))

    for o in around:
        signal(neighbours[o])
    partners = 0
    for group in [first] + mids:
        for mask in range(1, 2 ** len(group)):
            signal(partner(group, place, mask)[0])
            partners += 1

    @pl.when(jnp.logical_not(at_home))
    def _():
        signal(host(place, size_y))


    def lay_out(which):
        loads[which].wait()
        value = raw[which].astype(f32)
        planes = [value[:, :, z, :].reshape(64, 48) for z in range(2)]
        own[which] = jnp.concatenate(planes + [jnp.zeros((64, 32), f32)], axis=1).astype(bf16)

    lay_out(0)
    pl.semaphore_wait(barrier, 8 + partners + jnp.where(keeps, 8, 9) + jnp.where(at_home, 0, 1))

    outward = sorted(around, key=lambda o: -abs(o[0]) - abs(o[1]))

    def scatter(number, source):
        for o in outward + [(0, 0)]:
            target = near.at[number, 7 - around.index(o) if o != (0, 0) else 8]
            copy = pltpu.make_async_remote_copy(
                src_ref=source,
                dst_ref=target,
                send_sem=near_send.at[number],
                recv_sem=near_recv.at[number],
                device_id=targets[o],
                device_id_type=MESH,
            )
            if o[1]:
                copy.start()
            else:
                pl.when(jnp.logical_not(equal(targets[o], place)))(copy.start)

                @pl.when(equal(targets[o], place))
                def _():
                    pltpu.make_async_copy(source, target, near_recv.at[number]).start()

    def exchange(number, source):
        for o in outward:
            pltpu.make_async_remote_copy(
                src_ref=source,
                dst_ref=near.at[number, 7 - around.index(o)],
                send_sem=near_send.at[number],
                recv_sem=near_recv.at[number],
                device_id=neighbours[o],
                device_id_type=MESH,
            ).start()

    def send(number, block):
        sent[number] = block
        exchange(number, sent.at[number])

    def arrived(number):
        landed = near.at[number, pl.ds(0, 9 if number in (0, 6) else 8)]
        pltpu.make_async_copy(landed, landed, near_recv.at[number]).wait()

    def spread_out(slot, number, own, change):
        for i, j in offsets:
            block = own if (i, j) == (0, 0) else near[number, around.index((i, j))].astype(f32)
            region[slot, 8 * (i + 1) : 8 * (i + 2), 8 * (j + 2) : 8 * (j + 3), :] = change(
                block
            ).reshape(8, 8, 128)

    def rounded(value):
        return value.astype(bf16).astype(f32)

    def silu(value):
        return rounded(value * jax.nn.sigmoid(value))

    def slope(value):
        sigma = jax.nn.sigmoid(value)
        return sigma * (1.0 + value * (1.0 - sigma))

    def box(slot, x, y, extent_x, extent_y):
        return region[slot, x : x + extent_x, y + 8 : y + 8 + extent_y, :].reshape(
            extent_x * extent_y, 128
        )

    def put(slot, x, y, extent_x, extent_y, value):
        region[slot, x : x + extent_x, y + 8 : y + 8 + extent_y, :] = value.reshape(
            extent_x, extent_y, 128
        )

    def fill(slot, spread, x, y, extent_x, extent_y):
        rows = extent_x * extent_y
        for index, (i, j) in enumerate(offsets):
            cols[:rows, index * 128 : (index + 1) * 128] = box(
                slot, x + i * spread, y + j * spread, extent_x, extent_y
            ).astype(bf16)
        return rows

    def forward(layer, rows):
        return jnp.dot(cols[:rows], w_wide[layer], preferred_element_type=f32)

    def backward(layer, rows):
        return lax.dot_general(
            cols[:rows], w_side[layer], (((1,), (1,)), ((), ())), preferred_element_type=f32
        )

    lane = lax.broadcasted_iota(jnp.int32, (48, 128), 1)

    def roll(value, left):
        return pltpu.roll(value, (128 - left) % 128, 1) if left % 128 else value

    def pack(layer):
        group = 0 if layer in groups[0] else 1
        slot, layers, stage = groups[group].index(layer), len(groups[group]), stages[group]
        base = slot * layer_rows
        rest = None
        for index in range(9):
            shifted = cols[:64, index * 128 : (index + 1) * 128]
            piece = jnp.dot(turned[layer], shifted, preferred_element_type=f32)
            low, high = piece[:48], piece[48:96]
            moved = roll(high, 48)
            main = low + jnp.where((lane >= 48) & (lane < 96), 0.0, moved)
            stage[base + index * 48 : base + (index + 1) * 48] = main.astype(bf16)
            tail = jnp.where(lane < 16, high, 0.0)
            if index < 8:
                tail = roll(tail, 128 - 16 * index)
                rest = tail if rest is None else rest + tail
            else:
                last = roll(tail, 128 - 16 * slot)
        stage[base + 432 : base + 480] = rest.astype(bf16)
        shared = slice(layers * layer_rows, layers * layer_rows + 48)
        if slot:
            last = last + stage[shared].astype(f32)
        stage[shared] = last.astype(bf16)

    index1 = own_index(first, place)

    def piece_of(group, index):
        return pl.ds(pl.multiple_of(index * chunks[group], chunks[group]), chunks[group])

    def copies(group, phase, members, source, target):
        for mask in reversed(range(1, 2 ** len(members))):
            device, index = partner(members, place, mask)
            pltpu.make_async_remote_copy(
                src_ref=source(index),
                dst_ref=target(mask),
                send_sem=sum_send.at[group, phase],
                recv_sem=sum_recv.at[group, phase],
                device_id=device,
                device_id_type=MESH,
            ).start()

    def received(group, phase):
        if phase == 0:
            return lands[group]
        if phase < phases - 1:
            return mid_lands[group][phase - 1]
        return (packed1 if group else gathers[0]).at[pl.ds(0, (count1 - 1) * chunks[group])]

    def landed(group, phase):
        ref = received(group, phase)
        pltpu.make_async_copy(ref, ref, sum_recv.at[group, phase]).wait()

    def sum_send_first(group):
        copies(
            group, 0, first,
            lambda index: stages[group].at[piece_of(group, index)],
            lambda mask: lands[group].at[mask - 1],
        )

    def sum_step(group, phase):
        landed(group, phase)
        if phase == 0:
            terms = [stages[group][piece_of(group, index1)].astype(f32)]
            land, count = lands[group], count1
        else:
            terms = [parts[group][phase - 1][...].astype(f32)]
            land, count = mid_lands[group][phase - 1], 2 ** len(mids[phase - 1])
        terms += [land[mask - 1].astype(f32) for mask in range(1, count)]
        while len(terms) > 1:
            terms = [a + b for a, b in zip(terms[::2], terms[1::2])]
        total = terms[0].astype(bf16)
        if phase < len(mids):
            part = parts[group][phase]
            part[...] = total
            copies(
                group, phase + 1, mids[phase],
                lambda index: part,
                lambda mask: mid_lands[group][phase].at[mask - 1],
            )
        else:
            piece = pl.ds(0, chunks[group]) if group else piece_of(group, index1)
            gathers[group][piece] = total
            whole = gathers[group].at[piece]
            place_in = (packed1 if group else gathers[0]).at[piece_of(group, index1)]
            copies(group, phase + 1, first, lambda index: whole, lambda mask: place_in)
            if group:
                pltpu.make_async_copy(whole, place_in, out_sem.at[1]).start()

    scatter(0, own.at[0])
    lay_out(1)
    region[...] = jnp.zeros_like(region)
    w_wide[...] = jnp.zeros_like(w_wide)
    w_side[:, 96:] = jnp.zeros((7, 32, 1152), bf16)
    for group in range(2):
        used = len(groups[group]) * layer_rows + 48
        stages[group][used:] = jnp.zeros((group_rows[group] - used, 128), bf16)
    loads[2].wait()
    zeros32 = jnp.zeros((48, 32), f32)

    def widen(layer, carry):
        for index in range(9):
            minus, same, plus = (w_raw[layer, 3 * index + k].astype(f32) for k in range(3))
            low = jnp.concatenate([same, minus, zeros32], axis=1).astype(bf16)
            high = jnp.concatenate([plus, same, zeros32], axis=1).astype(bf16)
            w_wide[layer, index * 128 : index * 128 + 48] = low
            w_wide[layer, index * 128 + 48 : index * 128 + 96] = high
            w_side[layer, :48, index * 128 : (index + 1) * 128] = low
            w_side[layer, 48:96, index * 128 : (index + 1) * 128] = high
        return carry

    lax.fori_loop(0, 7, widen, 0)

    arrived(0)
    high0 = near[0, 8].astype(f32)
    acts[0] = silu(high0).astype(bf16)
    spread_out(0, 0, high0, lambda value: value)
    spread_out(1, 0, high0, silu)
    rows = fill(1, 1, 2, 0, 20, 24)
    scatter(6, own.at[1])
    value = rounded(box(0, 2, 0, 20, 24) + forward(0, rows))
    put(0, 2, 0, 20, 24, value)
    put(1, 2, 0, 20, 24, silu(value))
    high1[...] = box(0, 7, 4, 10, 16)
    acts[1] = box(1, 8, 8, 8, 8).astype(bf16)
    rows = fill(1, 2, 4, 4, 16, 16)
    value = rounded(box(0, 4, 4, 16, 16) + forward(1, rows))
    put(0, 4, 4, 16, 16, value)
    put(1, 4, 4, 16, 16, silu(value))
    high2[...] = box(0, 5, 4, 14, 16)
    acts[2] = box(1, 8, 8, 8, 8).astype(bf16)
    rows = fill(1, 4, 8, 8, 8, 8)
    high3 = rounded(box(0, 8, 8, 8, 8) + forward(2, rows))
    high_own[0] = high3
    active = silu(high3).astype(bf16)
    acts[3] = active
    send(1, active)
    arrived(1)

    def fill_blocks(number, own):
        for index, (i, j) in enumerate(offsets):
            block = own if (i, j) == (0, 0) else near[number, around.index((i, j))]
            cols[:64, index * 128 : (index + 1) * 128] = block

    fill_blocks(1, acts[3])
    high4 = rounded(high_own[0] + forward(3, 64))
    high_own[1] = high4
    send(2, high4.astype(bf16))
    acts[4] = silu(high4).astype(bf16)
    arrived(6)
    spread_out(2, 6, near[6, 8].astype(f32), lambda value: value)
    arrived(2)
    spread_out(0, 2, high_own[1], lambda value: value)
    spread_out(1, 2, high_own[1], silu)
    rows = fill(1, 4, 4, 4, 16, 16)
    value = rounded(box(0, 4, 4, 16, 16) + forward(4, rows))
    high5[...] = value
    put(0, 4, 4, 16, 16, value)
    put(1, 4, 4, 16, 16, silu(value))
    acts[5] = box(1, 8, 8, 8, 8).astype(bf16)
    rows = fill(1, 2, 8, 8, 8, 8)
    high6 = rounded(box(0, 8, 8, 8, 8) + forward(5, rows))
    high_own[2] = high6
    acts[6] = silu(high6).astype(bf16)

    def fill_back(slot, spread, x, y, extent_x, extent_y):
        return fill(slot, -spread, x, y, extent_x, extent_y)

    rows = fill_back(2, 1, 8, 8, 8, 8)
    grad6 = (near[6, 8].astype(f32) + slope(high_own[2]) * backward(6, rows)).astype(bf16)
    send(3, grad6)
    for layer in range(7):
        turned[layer] = jnp.transpose(acts[layer].astype(f32)).astype(bf16)
    pack(6)
    arrived(3)
    spread_out(2, 3, sent[3].astype(f32), lambda value: value)
    rows = fill_back(2, 2, 4, 4, 16, 16)
    value = rounded(box(2, 4, 4, 16, 16) + slope(high5[...]) * backward(5, rows))
    put(0, 4, 4, 16, 16, value)
    rows = fill_back(0, 4, 8, 8, 8, 8)
    grad4 = (box(0, 8, 8, 8, 8) + slope(high_own[1]) * backward(4, rows)).astype(bf16)
    send(4, grad4)
    pack(4)
    fill_back(2, 2, 8, 8, 8, 8)
    pack(5)
    sum_send_first(0)
    arrived(4)

    def fill_blocks_back(number, own):
        for index, (i, j) in enumerate(offsets):
            block = own if (i, j) == (0, 0) else near[number, around.index((-i, -j))]
            cols[:64, index * 128 : (index + 1) * 128] = block

    fill_blocks_back(4, sent[4])
    grad3 = (sent[4].astype(f32) + slope(high_own[0]) * backward(3, 64)).astype(bf16)
    send(5, grad3)
    pack(3)
    sum_step(0, 0)
    arrived(5)
    spread_out(2, 5, sent[5].astype(f32), lambda value: value)
    rows = fill_back(2, 4, 5, 4, 14, 16)
    value = rounded(box(2, 5, 4, 14, 16) + slope(high2[...]) * backward(2, rows))
    put(0, 5, 4, 14, 16, value)
    fill_back(2, 4, 8, 8, 8, 8)
    pack(2)
    rows = fill_back(0, 2, 7, 4, 10, 16)
    value = rounded(box(0, 7, 4, 10, 16) + slope(high1[...]) * backward(1, rows))
    put(1, 7, 4, 10, 16, value)
    fill_back(0, 2, 8, 8, 8, 8)
    pack(1)
    sum_step(0, 1)
    rows = fill_back(1, 1, 8, 8, 8, 8)
    pack(0)
    sum_send_first(1)
    back_home[...] = (
        box(1, 8, 8, 8, 8) + slope(near[0, 8].astype(f32)) * backward(0, rows)
    ).astype(bf16)
    to_owner = pltpu.make_async_remote_copy(
        src_ref=back_home,
        dst_ref=landed_home,
        send_sem=home_sem.at[0],
        recv_sem=home_sem.at[1],
        device_id=mine,
        device_id_type=MESH,
    )

    @pl.when(jnp.logical_not(at_home))
    def _():
        to_owner.start()

    @pl.when(at_home)
    def _():
        landed_home[...] = back_home[...]

    sum_step(1, 0)
    sum_step(0, 2)
    for phase in range(1, phases - 1):
        sum_step(1, phase)

    @pl.when(jnp.logical_not(at_home))
    def _():
        to_owner.wait()

    grad_store = pltpu.make_async_copy(landed_home, grad_any, raw_sem.at[0])
    grad_store.start()
    for number in range(1, 6):
        ref = near.at[number, pl.ds(0, 8)]
        pltpu.make_async_copy(ref, ref, near_send.at[number]).wait()
    for number in (0, 6):
        for count, chosen in ((8, keeps), (9, jnp.logical_not(keeps))):

            @pl.when(chosen)
            def _():
                ref = near.at[number, pl.ds(0, count)]
                pltpu.make_async_copy(ref, ref, near_send.at[number]).wait()

    landed(0, phases - 1)
    store = pltpu.make_async_copy(gathers[0], packed0, out_sem.at[0])
    store.start()
    own_piece = gathers[1].at[pl.ds(0, chunks[1])]
    pltpu.make_async_copy(own_piece, own_piece, out_sem.at[1]).wait()
    landed(1, phases - 1)
    for group in range(2):
        for phase in range(phases):
            ref = received(group, phase)
            pltpu.make_async_copy(ref, ref, sum_send.at[group, phase]).wait()
    store.wait()
    grad_store.wait()


def unpack(packed0, packed1, block_any, field_any, out_any, held0, held1, block, cells, wide, in_sem, out_sem):
    loads = [
        pltpu.make_async_copy(packed, held, in_sem.at[group])
        for group, (packed, held) in enumerate(((packed0, held0), (packed1, held1), (block_any, block)))
    ]
    for load in loads:
        load.start()
    stores = []
    lane = lax.broadcasted_iota(jnp.int32, (48, 128), 1)

    def roll(value, left):
        return pltpu.roll(value, (128 - left) % 128, 1) if left % 128 else value

    for group, held in enumerate((held0, held1)):
        loads[group].wait()
        if group:
            loads[2].wait()
            rows = block[...].astype(f32).reshape(8, 8, 128)
            cells[...] = jnp.stack([rows[:, :, :48], rows[:, :, 48:96]], axis=2).astype(bf16)
            stores.append(pltpu.make_async_copy(cells, field_any, out_sem.at[7]))
            stores[-1].start()
        shared = len(groups[group]) * layer_rows
        shared = held[shared : shared + 48].astype(f32)
        for slot, layer in enumerate(groups[group]):
            base = slot * layer_rows
            rest = held[base + 432 : base + 480].astype(f32)
            for index in range(9):
                main = held[base + index * 48 : base + (index + 1) * 48].astype(f32)
                tail = roll(rest, 16 * index) if index < 8 else roll(shared, 16 * slot)
                plus = jnp.where(lane < 16, tail, roll(main, 80))
                for k, value in enumerate((roll(main, 48), main, plus)):
                    wide[layer, 3 * index + k] = value[:, :48]
            stores.append(pltpu.make_async_copy(wide.at[layer], out_any.at[layer], out_sem.at[layer]))
            stores[-1].start()
    for store in stores:
        store.wait()


def on_device(field, cotangent, weights):
    size_x, size_y = lax.axis_size("gx"), lax.axis_size("gy")
    first, mids = plan(size_x, size_y)
    count1 = 2 ** len(first)
    far = pl.BlockSpec(memory_space=pl.ANY)
    buffers = []
    for rows in group_rows:
        chunk = rows // count1
        buffers += [
            pltpu.VMEM((rows, 128), bf16),
            pltpu.VMEM((count1 - 1, chunk, 128), bf16),
            pltpu.VMEM((rows, 128), bf16),
        ]
        for members in mids:
            buffers += [
                pltpu.VMEM((chunk, 128), bf16),
                pltpu.VMEM((2 ** len(members) - 1, chunk, 128), bf16),
            ]
    phases = len(mids) + 2
    grad, *sums = pl.pallas_call(
        functools.partial(kernel, size_x, size_y),
        out_shape=(
            jax.ShapeDtypeStruct((64, 128), bf16),
            *[jax.ShapeDtypeStruct((rows, 128), bf16) for rows in group_rows],
        ),
        in_specs=[far] * 3,
        out_specs=(far, far, far),
        scratch_shapes=[
            pltpu.VMEM((2,) + field.shape, bf16),
            pltpu.VMEM(weights.shape, bf16),
            pltpu.VMEM((2, 64, 128), bf16),
            pltpu.VMEM((7, 1152, 128), bf16),
            pltpu.VMEM((7, 128, 1152), bf16),
            pltpu.VMEM((7, 9, 64, 128), bf16),
            pltpu.VMEM((6, 64, 128), bf16),
            pltpu.VMEM((3, 24, 40, 128), f32),
            pltpu.VMEM((160, 128), f32),
            pltpu.VMEM((224, 128), f32),
            pltpu.VMEM((256, 128), f32),
            pltpu.VMEM((3, 64, 128), f32),
            pltpu.VMEM((7, 64, 128), bf16),
            pltpu.VMEM((7, 128, 64), bf16),
            pltpu.VMEM((480, 1152), bf16),
            pltpu.VMEM((64, 128), bf16),
            pltpu.VMEM((64, 128), bf16),
            *buffers,
            pltpu.SemaphoreType.DMA((3,)),
            pltpu.SemaphoreType.DMA((7,)),
            pltpu.SemaphoreType.DMA((7,)),
            pltpu.SemaphoreType.DMA((2,)),
            pltpu.SemaphoreType.DMA((2, phases)),
            pltpu.SemaphoreType.DMA((2, phases)),
            pltpu.SemaphoreType.DMA((2,)),
        ],
        compiler_params=pltpu.CompilerParams(
            collective_id=0, has_side_effects=True, vmem_limit_bytes=60 * 2**20
        ),
    )(field, cotangent, weights)
    return pl.pallas_call(
        unpack,
        out_shape=(
            jax.ShapeDtypeStruct(field.shape, bf16),
            jax.ShapeDtypeStruct(weights.shape, f32),
        ),
        in_specs=[far] * 3,
        out_specs=(far, far),
        scratch_shapes=[
            *[pltpu.VMEM((rows, 128), bf16) for rows in group_rows],
            pltpu.VMEM((64, 128), bf16),
            pltpu.VMEM(field.shape, bf16),
            pltpu.VMEM(weights.shape, f32),
            pltpu.SemaphoreType.DMA((3,)),
            pltpu.SemaphoreType.DMA((8,)),
        ],
        compiler_params=pltpu.CompilerParams(vmem_limit_bytes=60 * 2**20),
    )(*sums, grad)


def solution(mesh):
    in_specs = (P("gx", "gy", None, None), P("gx", "gy", None, None), P())
    out_specs = (P("gx", "gy", None, None), P())
    return jax.shard_map(
        on_device, mesh=mesh, in_specs=in_specs, out_specs=out_specs, check_vma=False
    )
```
